32 devices in a mesh: ex: 8 (over z, core), pd: 4 (over y, x).
Axes of the slice: x: 2, y: 2, z: 4, core: 2. Of those that a mesh axis runs over, the one named last changes fastest.
Arguments:
- verdict_states: bfloat16 [2048, 8192], P(('ex', 'pd')), may hold values from -6 to 6
- verdict_labels: int32 [64], replicated, may hold values from 0 to 1
- partner: int32 [64], replicated, may hold values from 0 to 63, as said below
- gate_weight: bfloat16 [8192, 28672], P(None, ('ex', 'pd')), may hold values from -0.0625 to 0.0625
- up_weight: bfloat16 [8192, 28672], P(None, ('ex', 'pd')), may hold values from -0.0625 to 0.0625
- down_weight: bfloat16 [28672, 8192], P(('ex', 'pd')), may hold values from -0.03125 to 0.03125
- readout: bfloat16 [8192], replicated, may hold values from -0.8984375 to 0.8984375
- sketch_in: bfloat16 [64, 8192], replicated, may hold values from -0.0625 to 0.0625
- sketch_out: bfloat16 [64, 28672], P(None, ('ex', 'pd')), may hold values from -6 to 6
- store: bfloat16 [65536, 4096], P('ex', 'pd'), may hold values from -0.099609375 to 0.099609375
- source_ids: int32 [65536], P('ex'), may hold values from 0 to 511
Outputs:
- contrast: float32 [64, 65536], P('pd', 'ex')
- source_scores: float32 [64, 512], P('pd')
The draws below stay inside these ranges and needn't reach their ends.
Inputs may be any that keep to these rules, and one draw needn't show every extreme that they name: partner[partner[r]] = r and partner[r] != r for every row r.
All inputs are finite; a program needn't handle non-finite values.
Results may differ from the reference program's by a relative error of at most 0.013.
Values may be sent and summed in bfloat16 or wider, within the bound.
No kernel may reach another device: no remote copies, remote signals or barrier semaphores. Data moves between devices by JAX's collectives and lax.ppermute only.
A program may use at most 192 MiB of HBM per device.

```python
import jax
import jax.numpy as jnp
from jax import lax

D = 8192
FF = 28672
KIN = 64
KOUT = 64
PROJ = 4096
ROWS = 64
LEN = 32
TOKENS = 2048
EXAMPLES = 65536
SOURCES = 512


def draw_partner(key, part):
    order = jax.random.permutation(key, ROWS).astype(jnp.int32)
    mates = order.reshape(ROWS // 2, 2)[:, ::-1].reshape(ROWS)
    return jnp.zeros((ROWS,), jnp.int32).at[order].set(mates)


def plant(entries, key, least, largest):
    spot = [jax.random.randint(jax.random.fold_in(key, axis), (), 0, length) for axis, length in enumerate(entries.shape)]
    widest = entries.shape.index(max(entries.shape))
    next_to = spot[:widest] + [(spot[widest] + 1) % entries.shape[widest]] + spot[widest + 1:]
    return entries.at[tuple(spot)].set(least).at[tuple(next_to)].set(largest)


def block_levels(key, shape, shards, smallest, largest):
    def one(position, blocks):
        draws = jax.random.uniform(jax.random.fold_in(jax.random.fold_in(key, 6), position), (blocks,), jnp.float32, smallest / len(shards), largest / len(shards))
        return jnp.repeat(jnp.exp(draws), shape[position] // blocks).reshape((-1,) + (1,) * (len(shape) - position - 1))

    gain = one(*shards[0])
    for cut in shards[1:]:
        gain = gain * one(*cut)
    return gain


def scatter_about(rng, extent, deviation, limit, cuts=(), dtype=jnp.bfloat16):
    factor_of = block_levels(rng, extent, cuts, -0.22, 0.18) if cuts else 1.0
    array = jax.random.normal(rng, extent, jnp.float32) * deviation * factor_of
    return jnp.minimum(jnp.maximum(array, -limit), limit).astype(dtype)


def setup_inputs(seed: int = 0) -> dict:
    streams_of = jax.random.split(jax.random.key(seed), 12)
    return {
        "verdict_states": scatter_about(streams_of[0], (TOKENS, D), 1.0, 6.0, ((0, 32),)),
        "verdict_labels": plant(jax.random.randint(streams_of[1], (ROWS,), 0, 2), jax.random.fold_in(streams_of[1], 1), 0, 1).astype(jnp.int32),
        "partner": draw_partner(jax.random.fold_in(streams_of[11], 71), 0),
        "gate_weight": scatter_about(streams_of[3], (D, FF), D ** -0.5, 0.0625, ((1, 32),)),
        "up_weight": scatter_about(streams_of[4], (D, FF), D ** -0.5, 0.0625, ((1, 32),)),
        "down_weight": scatter_about(streams_of[5], (FF, D), FF ** -0.5, 0.03125, ((0, 32),)),
        "readout": scatter_about(streams_of[6], (D,), 0.15, 0.8984375),
        "sketch_in": scatter_about(streams_of[7], (KIN, D), D ** -0.5, 0.0625),
        "sketch_out": scatter_about(streams_of[8], (KOUT, FF), 1.0, 6.0, ((1, 32),)),
        "store": scatter_about(streams_of[9], (EXAMPLES, PROJ), 0.015625, 0.099609375, ((0, 8), (1, 4))),
        "source_ids": plant(jax.random.randint(streams_of[10], (EXAMPLES,), 0, SOURCES), jax.random.fold_in(streams_of[10], 1), 0, SOURCES - 1).astype(jnp.int32),
    }


def reference(verdict_states, verdict_labels, partner, gate_weight, up_weight, down_weight, readout, sketch_in, sketch_out, store, source_ids):
    gate = jnp.dot(verdict_states, gate_weight, preferred_element_type=jnp.float32)
    up = jnp.dot(verdict_states, up_weight, preferred_element_type=jnp.float32)
    sig = jax.nn.sigmoid(gate)
    hidden = gate * sig * up
    pooled = hidden.reshape(ROWS, LEN, FF).sum(axis=1) / LEN
    wvec = jnp.dot(down_weight, readout, preferred_element_type=jnp.float32)
    logit = jnp.sum(pooled * wvec[None, :], axis=1)
    sign = 2.0 * verdict_labels.astype(jnp.float32) - 1.0
    coef = -sign * jax.nn.sigmoid(-sign * logit)
    scale_tok = jnp.repeat(coef / LEN, LEN)
    dgate = (scale_tok[:, None] * wvec[None, :] * up * sig * (1.0 + gate * (1.0 - sig))).astype(jnp.bfloat16)
    ain = lax.dot_general(verdict_states, sketch_in, (((1,), (1,)), ((), ())), preferred_element_type=jnp.float32)
    bout = lax.dot_general(dgate, sketch_out, (((1,), (1,)), ((), ())), preferred_element_type=jnp.float32)
    sketch = jnp.einsum("rti,rto->rio", ain.reshape(ROWS, LEN, KIN), bout.reshape(ROWS, LEN, KOUT), precision=lax.Precision.HIGHEST).reshape(ROWS, KIN * KOUT)
    diff = (sketch - sketch[partner]).astype(jnp.bfloat16)
    contrast = lax.dot_general(diff, store, (((1,), (1,)), ((), ())), preferred_element_type=jnp.float32)
    totals = jax.ops.segment_sum(contrast.T, source_ids, num_segments=SOURCES).T
    source_scores = totals * ((SOURCES / EXAMPLES) ** 0.5)
    return contrast, source_scores
```

```python
import math

import jax
import jax.numpy as jnp
from jax import lax
from jax.sharding import PartitionSpec as P

SOURCES = 512
CORES = 2
CONTRACT = (((1,), (1,)), ((), ()))


def swap(value, axis, mask):
    size = lax.axis_size(axis)
    return lax.ppermute(value, axis, [(i, i ^ mask) for i in range(size)])


def turn(value, axis, shift):
    size = lax.axis_size(axis)
    return lax.ppermute(value, axis, [(i, (i + shift) % size) for i in range(size)])


def pick(value, index, axis):
    return lax.dynamic_index_in_dim(value, index, axis, keepdims=False)


def source_table(store, source_ids):
    onehot = (source_ids[None, :] == jnp.arange(SOURCES, dtype=jnp.int32)[:, None]).astype(
        jnp.bfloat16
    )
    return jnp.dot(onehot, store, preferred_element_type=jnp.float32)


def reduce_rows(part):
    rows, parts, width = part.shape
    me, pd = lax.axis_index("ex"), lax.axis_index("pd")
    core = me % CORES
    halves = part.reshape(CORES, rows // CORES, parts, width)
    half = pick(halves, core, 0) + swap(pick(halves, 1 - core, 0), "ex", 1)
    total = pick(half, pd, 1)
    for k in range(1, parts):
        total = total + swap(pick(half, pd ^ k, 1), "pd", k)
    chips = lax.axis_size("ex") // CORES
    whole = total
    for k in range(1, chips):
        whole = whole + turn(total, "ex", CORES * k)
    other = swap(whole, "ex", 1)
    first = jnp.where(core == 0, whole, other)
    second = jnp.where(core == 0, other, whole)
    return jnp.concatenate([first, second], axis=0)


def sum_scores(part, mine):
    rows, sources = part.shape
    parts = rows // mine
    pd = lax.axis_index("pd")
    blocks = part.reshape(parts, mine, sources)
    total = pick(blocks, pd, 0)
    for k in range(1, parts):
        total = total + swap(pick(blocks, pd ^ k, 0), "pd", k)
    chips = lax.axis_size("ex") // CORES
    whole = total
    for k in range(1, chips):
        whole = whole + turn(total, "ex", CORES * k)
    return whole + swap(whole, "ex", 1)


def sum_contrast(part, mine):
    rows, examples = part.shape
    parts = rows // mine
    pd = lax.axis_index("pd")
    blocks = part.reshape(parts, mine, examples)
    total = pick(blocks, pd, 0).astype(jnp.float32)
    for k in range(1, parts):
        total = total + swap(pick(blocks, pd ^ k, 0), "pd", k).astype(jnp.float32)
    return total


def on_device(
    verdict_states,
    verdict_labels,
    partner,
    gate_weight,
    up_weight,
    down_weight,
    readout,
    sketch_in,
    sketch_out,
    store,
    source_ids,
):
    kin = sketch_in.shape[0]
    kout = sketch_out.shape[0]
    rows = verdict_labels.shape[0]
    ff_local = gate_weight.shape[1]
    parts = lax.axis_size("pd")
    width = store.shape[1]

    states = lax.all_gather(verdict_states, ("ex", "pd"), axis=0, tiled=True)
    wvec = jnp.dot(down_weight, readout, preferred_element_type=jnp.float32)
    table = source_table(store, source_ids)

    gate = jnp.dot(states, gate_weight, preferred_element_type=jnp.float32)
    up = jnp.dot(states, up_weight, preferred_element_type=jnp.float32)
    ain = lax.dot_general(states, sketch_in, CONTRACT, preferred_element_type=jnp.float32)
    tokens = gate.shape[0]
    length = tokens // rows
    sig = jax.nn.sigmoid(gate)
    weighted = up * wvec[None, :]
    logit = jnp.sum((gate * sig * weighted).reshape(rows, length * ff_local), axis=1) / length
    dgate = (weighted * sig * (1.0 + gate * (1.0 - sig)) / length).astype(jnp.bfloat16)
    bout = lax.dot_general(dgate, sketch_out, CONTRACT, preferred_element_type=jnp.float32)
    sketch = jnp.einsum(
        "rti,rto->rio",
        ain.reshape(rows, length, kin),
        bout.reshape(rows, length, kout),
        precision=lax.Precision.HIGHEST,
    ).reshape(rows, parts, width)
    tail = jnp.broadcast_to(logit[:, None, None], (rows, parts, 128))
    reduced = reduce_rows(jnp.concatenate([sketch, tail], axis=2))

    sign = 2.0 * verdict_labels.astype(jnp.float32) - 1.0
    coef = -sign * jax.nn.sigmoid(-sign * reduced[:, width])
    scaled = reduced[:, :width] * coef[:, None]
    diff = (scaled - scaled[partner]).astype(jnp.bfloat16)

    mine = rows // parts
    table_high = table.astype(jnp.bfloat16)
    table_low = (table - table_high.astype(jnp.float32)).astype(jnp.bfloat16)
    score_part = lax.dot_general(
        diff, table_high, CONTRACT, preferred_element_type=jnp.float32
    ) + lax.dot_general(diff, table_low, CONTRACT, preferred_element_type=jnp.float32)
    factor = (SOURCES / (store.shape[0] * lax.axis_size("ex"))) ** 0.5
    scores = sum_scores(score_part * factor, mine)
    contrast_part = lax.dot_general(
        diff, store, CONTRACT, preferred_element_type=jnp.float32
    ).astype(jnp.bfloat16)
    contrast = sum_contrast(contrast_part, mine)
    return (contrast, scores)


def solution(mesh):
    in_specs = (
        P(("ex", "pd"), None),
        P(),
        P(),
        P(None, ("ex", "pd")),
        P(None, ("ex", "pd")),
        P(("ex", "pd"), None),
        P(),
        P(),
        P(None, ("ex", "pd")),
        P("ex", "pd"),
        P("ex"),
    )
    out_specs = (P("pd", "ex"), P("pd", None))
    return jax.shard_map(
        on_device, mesh=mesh, in_specs=in_specs, out_specs=out_specs, check_vma=False
    )
```

```python
import functools

import jax
import jax.numpy as jnp
from jax import lax
from jax.experimental import pallas as pl
from jax.experimental.pallas import tpu as pltpu
from jax.sharding import PartitionSpec as P

SOURCES = 512
CORES = 2
CONTRACT = (((1,), (1,)), ((), ()))


def swap(value, axis, mask):
    size = lax.axis_size(axis)
    return lax.ppermute(value, axis, [(i, i ^ mask) for i in range(size)])


def turn(value, axis, shift):
    size = lax.axis_size(axis)
    return lax.ppermute(value, axis, [(i, (i + shift) % size) for i in range(size)])


def pick(value, index, axis):
    return lax.dynamic_index_in_dim(value, index, axis, keepdims=False)


def source_table(store, source_ids):
    onehot = (source_ids[None, :] == jnp.arange(SOURCES, dtype=jnp.int32)[:, None]).astype(
        jnp.bfloat16
    )
    return jnp.dot(onehot, store, preferred_element_type=jnp.float32)


def reduce_rows(part):
    rows, parts, width = part.shape
    me, pd = lax.axis_index("ex"), lax.axis_index("pd")
    core = me % CORES
    halves = part.reshape(CORES, rows // CORES, parts, width)
    half = pick(halves, core, 0) + swap(pick(halves, 1 - core, 0), "ex", 1)
    total = pick(half, pd, 1)
    for k in range(1, parts):
        total = total + swap(pick(half, pd ^ k, 1), "pd", k)
    chips = lax.axis_size("ex") // CORES
    whole = total
    for k in range(1, chips):
        whole = whole + turn(total, "ex", CORES * k)
    other = swap(whole, "ex", 1)
    first = jnp.where(core == 0, whole, other)
    second = jnp.where(core == 0, other, whole)
    return jnp.concatenate([first, second], axis=0)


def sum_scores(part, mine):
    rows, sources = part.shape
    parts = rows // mine
    pd = lax.axis_index("pd")
    blocks = part.reshape(parts, mine, sources)
    total = pick(blocks, pd, 0)
    for k in range(1, parts):
        total = total + swap(pick(blocks, pd ^ k, 0), "pd", k)
    chips = lax.axis_size("ex") // CORES
    whole = total
    for k in range(1, chips):
        whole = whole + turn(total, "ex", CORES * k)
    return whole + swap(whole, "ex", 1)


def sum_contrast(part, mine):
    rows, examples = part.shape
    parts = rows // mine
    pd = lax.axis_index("pd")
    blocks = part.reshape(parts, mine, examples)
    total = pick(blocks, pd, 0).astype(jnp.float32)
    for k in range(1, parts):
        total = total + swap(pick(blocks, pd ^ k, 0), "pd", k).astype(jnp.float32)
    return total


def plane_perm(masks):
    parts = lax.axis_size("pd")
    return [
        (ex * parts + pd, ex * parts + (pd ^ masks[ex % CORES]))
        for ex in range(lax.axis_size("ex"))
        for pd in range(parts)
    ]


def layer_kernel(count, length, *refs):
    pieces = refs[:count]
    gate_w, up_w, sin, sout, wvec, ain, bout, lrow, x, acc_g, acc_u = refs[count:]
    step = pl.program_id(0)
    tokens = pieces[0].shape[0]
    for i, piece in enumerate(pieces):
        x[i * tokens : (i + 1) * tokens, :] = piece[...]

    @pl.when(step == 0)
    def _():
        acc_g[...] = jnp.zeros_like(acc_g)
        acc_u[...] = jnp.zeros_like(acc_u)
        ain[...] = jnp.zeros_like(ain)

    acc_g[...] += jnp.dot(x[...], gate_w[...], preferred_element_type=jnp.float32)
    acc_u[...] += jnp.dot(x[...], up_w[...], preferred_element_type=jnp.float32)
    ain[...] += lax.dot_general(x[...], sin[...], CONTRACT, preferred_element_type=jnp.float32)

    @pl.when(step == pl.num_programs(0) - 1)
    def _():
        features = acc_g.shape[1]
        chunk = 2 * length
        groups = length // 8
        for i in range(acc_g.shape[0] // chunk):
            here = pl.ds(i * chunk, chunk)
            gate = acc_g[here, :]
            weighted = acc_u[here, :] * wvec[...]
            sig = jax.nn.sigmoid(gate)
            hidden = gate * sig * weighted
            total = hidden[:, :128]
            for j in range(1, features // 128):
                total = total + hidden[:, j * 128 : (j + 1) * 128]
            total = total.reshape(2, groups, 8, 128).sum(axis=1)
            lrow[pl.ds(16 * i, 16), :] = total.reshape(16, 128)
            dgate = (weighted * sig * (1.0 + gate * (1.0 - sig)) * (1.0 / length)).astype(
                jnp.bfloat16
            )
            bout[here, :] = lax.dot_general(
                dgate, sout[...], CONTRACT, preferred_element_type=jnp.float32
            )


def layer(pieces, gate_weight, up_weight, sketch_in, sketch_out, wvec, length):
    count = len(pieces)
    tokens, depth = pieces[0].shape
    features = gate_weight.shape[1]
    kin, kout = sketch_in.shape[0], sketch_out.shape[0]
    total = count * tokens
    rows = total // length
    block = min(1024, depth)
    ain, bout, lrow = pl.pallas_call(
        functools.partial(layer_kernel, count, length),
        grid=(depth // block,),
        in_specs=[pl.BlockSpec((tokens, block), lambda k: (0, k))] * count
        + [
            pl.BlockSpec((block, features), lambda k: (k, 0)),
            pl.BlockSpec((block, features), lambda k: (k, 0)),
            pl.BlockSpec((kin, block), lambda k: (0, k)),
            pl.BlockSpec((kout, features), lambda k: (0, 0)),
            pl.BlockSpec((1, features), lambda k: (0, 0)),
        ],
        out_specs=[
            pl.BlockSpec((total, kin), lambda k: (0, 0)),
            pl.BlockSpec((total, kout), lambda k: (0, 0)),
            pl.BlockSpec((rows * 8, 128), lambda k: (0, 0)),
        ],
        out_shape=[
            jax.ShapeDtypeStruct((total, kin), jnp.float32),
            jax.ShapeDtypeStruct((total, kout), jnp.float32),
            jax.ShapeDtypeStruct((rows * 8, 128), jnp.float32),
        ],
        scratch_shapes=[
            pltpu.VMEM((total, block), jnp.bfloat16),
            pltpu.VMEM((total, features), jnp.float32),
            pltpu.VMEM((total, features), jnp.float32),
        ],
        compiler_params=pltpu.CompilerParams(vmem_limit_bytes=48 * 1024 * 1024),
        cost_estimate=pl.CostEstimate(
            flops=2 * total * depth * (2 * features + kin),
            bytes_accessed=2 * depth * (2 * features + total),
            transcendentals=total * features,
        ),
    )(*pieces, gate_weight, up_weight, sketch_in, sketch_out, wvec)
    logit = lrow.reshape(rows, 8 * 128).sum(axis=1) / length
    sketch = jnp.einsum(
        "rti,rto->rio",
        ain.reshape(rows, length, kin),
        bout.reshape(rows, length, kout),
        precision=lax.Precision.HIGHEST,
    ).reshape(rows, kin * kout)
    return sketch, logit


def add_logit(sketch, logit, parts):
    rows = sketch.shape[0]
    wide = jnp.broadcast_to(logit[:, None, None], (rows, parts, 128))
    return jnp.concatenate([sketch.reshape(rows, parts, -1), wide], axis=2)


def plane_sum(part):
    rows, parts, width = part.shape
    core, pd = lax.axis_index("ex") % CORES, lax.axis_index("pd")
    halves = part.reshape(CORES, rows // CORES, parts, width)
    half = pick(halves, core, 0) + swap(pick(halves, 1 - core, 0), "ex", 1)
    total = pick(half, pd, 1)
    for k in range(1, parts):
        total = total + swap(pick(half, pd ^ k, 1), "pd", k)
    return total


def piped_sketches(
    states, gate_weight, up_weight, wvec, table, sketch_in, sketch_out, rows
):
    parts = lax.axis_size("pd")
    chips = lax.axis_size("ex") // CORES
    core, pd = lax.axis_index("ex") % CORES, lax.axis_index("pd")
    place = lax.axis_index("ex") // CORES
    mine = states.shape[0]
    length = mine * parts * CORES * chips // rows
    first, second = (2, 1), (1, 2)
    both = ("ex", "pd")

    def sibling(value):
        return swap(value, "ex", 1)

    cores = jnp.arange(CORES)[:, None]
    apart = jnp.arange(parts)[None, :] ^ pd
    here = jnp.where(cores == 0, apart == first[0], apart == first[1])
    base = jnp.where(apart == 0, 0, jnp.where(apart == 3, 6, jnp.where(here, 2, 4)))
    slot = (base + (cores != core)).reshape(-1)

    run = functools.partial(
        layer,
        gate_weight=gate_weight,
        up_weight=up_weight,
        sketch_in=sketch_in,
        sketch_out=sketch_out,
        wvec=wvec,
        length=length,
    )
    sums = []
    here = states
    for step in range(chips):
        a = lax.ppermute(here, both, plane_perm(first))
        b = lax.ppermute(here, both, plane_perm(second))
        later = turn(here, "ex", CORES) if step < chips - 1 else None
        d = lax.ppermute(a, both, plane_perm(second))
        early = [here, sibling(here), a, sibling(a), b, sibling(b)]
        late = [d, sibling(d)]
        if step < chips - 1:
            if step == 1:
                early[0], table = lax.optimization_barrier((early[0], table))
            sketch, logit = run(early + late)
        else:
            (s0, l0), (s1, l1) = run(early), run(late)
            sketch, logit = jnp.concatenate([s0, s1]), jnp.concatenate([l0, l1])
        part = add_logit(sketch, logit, parts)
        part = part.reshape(CORES * parts, -1, *part.shape[1:])[slot]
        sums.append(plane_sum(part.reshape(-1, *part.shape[2:])))
        here = later
    early, late = jnp.stack(sums[:-1]), sums[-1]
    got = [
        (early, late)
        if k == 0
        else (turn(early, "ex", CORES * k), turn(late, "ex", CORES * k))
        for k in range(chips)
    ]
    whole = []
    for j in range(chips):
        terms = []
        for k in range(chips):
            r = (j - k) % chips
            terms.append(got[k][1] if r == chips - 1 else got[k][0][r])
        whole.append(sum(terms))
    whole = jnp.stack(whole)[(place - jnp.arange(chips)) % chips]
    other = sibling(whole)
    low = jnp.where(core == 0, whole, other)
    high = jnp.where(core == 0, other, whole)
    return jnp.stack([low, high], axis=1).reshape(rows, -1), table


def plain_sketches(
    states, gate_weight, up_weight, wvec, table, sketch_in, sketch_out, rows
):
    kin, kout = sketch_in.shape[0], sketch_out.shape[0]
    ff_local = gate_weight.shape[1]
    states = lax.all_gather(states, ("ex", "pd"), axis=0, tiled=True)
    gate = jnp.dot(states, gate_weight, preferred_element_type=jnp.float32)
    up = jnp.dot(states, up_weight, preferred_element_type=jnp.float32)
    ain = lax.dot_general(states, sketch_in, CONTRACT, preferred_element_type=jnp.float32)
    length = states.shape[0] // rows
    sig = jax.nn.sigmoid(gate)
    weighted = up * wvec
    logit = jnp.sum((gate * sig * weighted).reshape(rows, length * ff_local), axis=1) / length
    dgate = (weighted * sig * (1.0 + gate * (1.0 - sig)) / length).astype(jnp.bfloat16)
    bout = lax.dot_general(dgate, sketch_out, CONTRACT, preferred_element_type=jnp.float32)
    sketch = jnp.einsum(
        "rti,rto->rio",
        ain.reshape(rows, length, kin),
        bout.reshape(rows, length, kout),
        precision=lax.Precision.HIGHEST,
    ).reshape(rows, kin * kout)
    return reduce_rows(add_logit(sketch, logit, lax.axis_size("pd"))), table


def on_device(
    verdict_states,
    verdict_labels,
    partner,
    gate_weight,
    up_weight,
    down_weight,
    readout,
    sketch_in,
    sketch_out,
    store,
    source_ids,
):
    rows = verdict_labels.shape[0]
    parts = lax.axis_size("pd")
    devices = parts * lax.axis_size("ex")
    width = store.shape[1]
    mine = verdict_states.shape[0]
    length = mine * devices // rows

    wvec = jnp.dot(down_weight, readout, preferred_element_type=jnp.float32)[None, :]
    table = source_table(store, source_ids)
    piped = (
        parts == 4
        and lax.axis_size("ex") % CORES == 0
        and mine % (2 * length) == 0
        and length % 8 == 0
        and gate_weight.shape[1] % 128 == 0
        and gate_weight.shape[0] % 1024 == 0
    )
    sketches = piped_sketches if piped else plain_sketches
    reduced, table = sketches(
        verdict_states, gate_weight, up_weight, wvec, table, sketch_in, sketch_out, rows
    )

    sign = 2.0 * verdict_labels.astype(jnp.float32) - 1.0
    coef = -sign * jax.nn.sigmoid(-sign * reduced[:, width])
    scaled = reduced[:, :width] * coef[:, None]
    diff = (scaled - scaled[partner]).astype(jnp.bfloat16)

    mine = rows // parts
    table_high = table.astype(jnp.bfloat16)
    table_low = (table - table_high.astype(jnp.float32)).astype(jnp.bfloat16)
    score_part = lax.dot_general(
        diff, table_high, CONTRACT, preferred_element_type=jnp.float32
    ) + lax.dot_general(diff, table_low, CONTRACT, preferred_element_type=jnp.float32)
    factor = (SOURCES / (store.shape[0] * lax.axis_size("ex"))) ** 0.5
    scores = sum_scores(score_part * factor, mine)
    contrast_part = lax.dot_general(
        diff, store, CONTRACT, preferred_element_type=jnp.float32
    ).astype(jnp.bfloat16)
    contrast = sum_contrast(contrast_part, mine)
    return (contrast, scores)


def solution(mesh):
    in_specs = (
        P(("ex", "pd"), None),
        P(),
        P(),
        P(None, ("ex", "pd")),
        P(None, ("ex", "pd")),
        P(("ex", "pd"), None),
        P(),
        P(),
        P(None, ("ex", "pd")),
        P("ex", "pd"),
        P("ex"),
    )
    out_specs = (P("pd", "ex"), P("pd", None))
    return jax.shard_map(
        on_device, mesh=mesh, in_specs=in_specs, out_specs=out_specs, check_vma=False
    )
```

```python
import functools

import jax
import jax.numpy as jnp
from jax import lax
from jax.experimental import pallas as pl
from jax.experimental.pallas import tpu as pltpu
from jax.sharding import Mesh
from jax.sharding import PartitionSpec as P

SOURCES = 512
CORES = 2
CONTRACT = (((1,), (1,)), ((), ()))


def swap(value, axis, mask):
    size = lax.axis_size(axis)
    return lax.ppermute(value, axis, [(i, i ^ mask) for i in range(size)])


def turn(value, axis, shift):
    size = lax.axis_size(axis)
    return lax.ppermute(value, axis, [(i, (i + shift) % size) for i in range(size)])


def pick(value, index, axis):
    return lax.dynamic_index_in_dim(value, index, axis, keepdims=False)


def source_table(store, source_ids):
    onehot = (source_ids[None, :] == jnp.arange(SOURCES, dtype=jnp.int32)[:, None]).astype(
        jnp.bfloat16
    )
    return jnp.dot(onehot, store, preferred_element_type=jnp.float32)


def reduce_rows(part):
    rows, parts, width = part.shape
    core, pd = lax.axis_index("core"), lax.axis_index("pd")
    halves = part.reshape(CORES, rows // CORES, parts, width)
    half = pick(halves, core, 0) + swap(pick(halves, 1 - core, 0), "core", 1)
    total = pick(half, pd, 1)
    for k in range(1, parts):
        total = total + swap(pick(half, pd ^ k, 1), "pd", k)
    whole = total
    for k in range(1, lax.axis_size("chip")):
        whole = whole + turn(total, "chip", k)
    other = swap(whole, "core", 1)
    first = jnp.where(core == 0, whole, other)
    second = jnp.where(core == 0, other, whole)
    return jnp.concatenate([first, second], axis=0)


def sum_scores(part, mine):
    rows, sources = part.shape
    parts = rows // mine
    pd = lax.axis_index("pd")
    blocks = part.reshape(parts, mine, sources)
    total = pick(blocks, pd, 0)
    for k in range(1, parts):
        total = total + swap(pick(blocks, pd ^ k, 0), "pd", k)
    whole = total
    for k in range(1, lax.axis_size("chip")):
        whole = whole + turn(total, "chip", k)
    return whole + swap(whole, "core", 1)


def sum_contrast(part, mine):
    rows, examples = part.shape
    parts = rows // mine
    pd = lax.axis_index("pd")
    blocks = part.reshape(parts, mine, examples)
    total = pick(blocks, pd, 0).astype(jnp.float32)
    for k in range(1, parts):
        total = total + swap(pick(blocks, pd ^ k, 0), "pd", k).astype(jnp.float32)
    return total


def layer_kernel(count, length, *refs):
    pieces = refs[:count]
    gate_w, up_w, sin, sout, wvec, ain, bout, lrow, x, w, acc, sems = refs[count:]
    step = pl.program_id(0)
    steps = pl.num_programs(0)
    block = x.shape[1]
    features = gate_w.shape[1]

    def copies(k):
        slot = lax.rem(k, 2)
        here = pl.ds(pl.multiple_of(k * block, block), block)
        return [
            pltpu.make_async_copy(
                weight.at[here, :],
                w.at[slot, :, pl.ds(i * features, features)],
                sems.at[slot, i],
            )
            for i, weight in enumerate((gate_w, up_w))
        ]

    @pl.when(step == 0)
    def _():
        for copy in copies(step):
            copy.start()
        acc[...] = jnp.zeros_like(acc)
        ain[...] = jnp.zeros_like(ain)

    @pl.when(step + 1 < steps)
    def _():
        for copy in copies(step + 1):
            copy.start()

    tokens = pieces[0].shape[0]
    for i, piece in enumerate(pieces):
        x[i * tokens : (i + 1) * tokens, :] = piece[...]
    for copy in copies(step):
        copy.wait()
    ain[...] += lax.dot_general(x[...], sin[...], CONTRACT, preferred_element_type=jnp.float32)
    acc[...] += jnp.dot(x[...], w[lax.rem(step, 2)], preferred_element_type=jnp.float32)

    @pl.when(step == steps - 1)
    def _():
        chunk = 64
        groups = length // 8
        rows = chunk // length
        for i in range(acc.shape[0] // chunk):
            here = pl.ds(i * chunk, chunk)
            gate = acc[here, :features]
            weighted = acc[here, features:] * wvec[...]
            sig = jax.nn.sigmoid(gate)
            hidden = gate * sig * weighted
            total = hidden[:, :128]
            for j in range(1, features // 128):
                total = total + hidden[:, j * 128 : (j + 1) * 128]
            total = total.reshape(rows, groups, 8, 128).sum(axis=1)
            lrow[pl.ds(8 * rows * i, 8 * rows), :] = total.reshape(8 * rows, 128)
            dgate = (weighted * sig * (1.0 + gate * (1.0 - sig))).astype(jnp.bfloat16)
            bout[here, :] = lax.dot_general(
                dgate, sout[...], CONTRACT, preferred_element_type=jnp.float32
            )


def layer(pieces, gate_weight, up_weight, sketch_in, sketch_out, wvec, length):
    count = len(pieces)
    tokens, depth = pieces[0].shape
    total = count * tokens
    features = gate_weight.shape[1]
    kin, kout = sketch_in.shape[0], sketch_out.shape[0]
    rows = total // length
    block = min(1024, depth)
    ain, bout, lrow = pl.pallas_call(
        functools.partial(layer_kernel, count, length),
        grid=(depth // block,),
        in_specs=[pl.BlockSpec((tokens, block), lambda k: (0, k))] * count
        + [
            pl.BlockSpec(memory_space=pl.ANY),
            pl.BlockSpec(memory_space=pl.ANY),
            pl.BlockSpec((kin, block), lambda k: (0, k)),
            pl.BlockSpec((kout, features), lambda k: (0, 0)),
            pl.BlockSpec((1, features), lambda k: (0, 0)),
        ],
        out_specs=[
            pl.BlockSpec((total, kin), lambda k: (0, 0)),
            pl.BlockSpec((total, kout), lambda k: (0, 0)),
            pl.BlockSpec((rows * 8, 128), lambda k: (0, 0)),
        ],
        out_shape=[
            jax.ShapeDtypeStruct((total, kin), jnp.float32),
            jax.ShapeDtypeStruct((total, kout), jnp.float32),
            jax.ShapeDtypeStruct((rows * 8, 128), jnp.float32),
        ],
        scratch_shapes=[
            pltpu.VMEM((total, block), jnp.bfloat16),
            pltpu.VMEM((2, block, 2 * features), jnp.bfloat16),
            pltpu.VMEM((total, 2 * features), jnp.float32),
            pltpu.SemaphoreType.DMA((2, 2)),
        ],
        compiler_params=pltpu.CompilerParams(vmem_limit_bytes=60 * 1024 * 1024),
        cost_estimate=pl.CostEstimate(
            flops=2 * total * depth * (2 * features + kin),
            bytes_accessed=2 * depth * (2 * features + total),
            transcendentals=total * features,
        ),
    )(*pieces, gate_weight, up_weight, sketch_in, sketch_out, wvec)
    logit = lrow.reshape(rows, 8 * 128).sum(axis=1)
    sketch = jnp.einsum(
        "rti,rto->rio",
        ain.reshape(rows, length, kin),
        bout.reshape(rows, length, kout),
        precision=lax.Precision.HIGHEST,
    ).reshape(rows, kin * kout)
    return sketch, logit


def add_logit(sketch, logit, parts):
    rows = sketch.shape[0]
    wide = jnp.broadcast_to(logit[:, None, None], (rows, parts, 128))
    return jnp.concatenate([sketch.reshape(rows, parts, -1), wide], axis=2)


def sibling(value):
    return swap(value, "core", 1)


def sum_rows(own, other):
    parts = own.shape[1]
    pd = lax.axis_index("pd")
    half = own + sibling(other)
    total = pick(half, pd, 1)
    for k in range(1, parts):
        total = total + swap(pick(half, pd ^ k, 1), "pd", k)
    whole = total
    for k in range(1, lax.axis_size("chip")):
        whole = whole + turn(total, "chip", k)
    return whole, sibling(whole)


def piped_sketches(
    states, gate_weight, up_weight, wvec, table, sketch_in, sketch_out, rows, length
):
    parts = lax.axis_size("pd")
    core = lax.axis_index("core")
    mine, depth = states.shape
    piece = 16
    pieces = mine // piece
    gathered = [
        lax.all_gather(
            states[j * piece : (j + 1) * piece], ("chip", "pd"), axis=0, tiled=True
        )
        for j in range(pieces)
    ]
    run = functools.partial(
        layer,
        gate_weight=gate_weight,
        up_weight=up_weight,
        sketch_in=sketch_in,
        sketch_out=sketch_out,
        wvec=wvec,
        length=min(piece, length),
    )
    per_row = length // piece
    results = []
    own_sum = other_sum = None
    done = table
    for j in range(pieces):
        block, done = lax.optimization_barrier((gathered[j], done))
        if j == 0:
            table = done
        swapped = sibling(block)
        if j < pieces - 1:
            both = run([block, swapped])
            done = both
            half = both[0].shape[0] // 2
            own, other = [p[:half] for p in both], [p[half:] for p in both]
        else:
            own, other = run([block]), run([swapped])
        if j % per_row == 0:
            own_sum, other_sum = own, other
        else:
            own_sum = [p + q for p, q in zip(own_sum, own)]
            other_sum = [p + q for p, q in zip(other_sum, other)]
        if j % per_row == per_row - 1:
            results.append(
                sum_rows(add_logit(*own_sum, parts), add_logit(*other_sum, parts))
            )
            done = (done, results[-1])
    own = jnp.stack([r[0] for r in results], axis=1)
    other = jnp.stack([r[1] for r in results], axis=1)
    shape = (lax.axis_size("chip"), 1, -1, own.shape[2])
    own, other = own.reshape(shape), other.reshape(shape)
    low = jnp.where(core == 0, own, other)
    high = jnp.where(core == 0, other, own)
    reduced = jnp.concatenate([low, high], axis=1).reshape(rows, -1)
    return reduced.at[:, -128:].multiply(1.0 / length), 1.0 / length, table


def plain_sketches(
    states, gate_weight, up_weight, wvec, table, sketch_in, sketch_out, rows, length
):
    kin, kout = sketch_in.shape[0], sketch_out.shape[0]
    ff_local = gate_weight.shape[1]
    states = lax.all_gather(states, ("chip", "core", "pd"), axis=0, tiled=True)
    gate = jnp.dot(states, gate_weight, preferred_element_type=jnp.float32)
    up = jnp.dot(states, up_weight, preferred_element_type=jnp.float32)
    ain = lax.dot_general(states, sketch_in, CONTRACT, preferred_element_type=jnp.float32)
    sig = jax.nn.sigmoid(gate)
    weighted = up * wvec
    logit = jnp.sum((gate * sig * weighted).reshape(rows, length * ff_local), axis=1) / length
    dgate = (weighted * sig * (1.0 + gate * (1.0 - sig)) / length).astype(jnp.bfloat16)
    bout = lax.dot_general(dgate, sketch_out, CONTRACT, preferred_element_type=jnp.float32)
    sketch = jnp.einsum(
        "rti,rto->rio",
        ain.reshape(rows, length, kin),
        bout.reshape(rows, length, kout),
        precision=lax.Precision.HIGHEST,
    ).reshape(rows, kin * kout)
    return reduce_rows(add_logit(sketch, logit, lax.axis_size("pd"))), 1.0, table


def on_device(
    verdict_states,
    verdict_labels,
    partner,
    gate_weight,
    up_weight,
    down_weight,
    readout,
    sketch_in,
    sketch_out,
    store,
    source_ids,
):
    rows = verdict_labels.shape[0]
    parts = lax.axis_size("pd")
    devices = parts * CORES * lax.axis_size("chip")
    width = store.shape[1]
    mine = verdict_states.shape[0]
    length = mine * devices // rows

    wvec = jnp.dot(down_weight, readout, preferred_element_type=jnp.float32)[None, :]
    table = source_table(store, source_ids)
    piped = (
        mine % 16 == 0
        and length % 16 == 0
        and mine % length == 0
        and parts * lax.axis_size("chip") % 4 == 0
        and gate_weight.shape[1] % 128 == 0
        and gate_weight.shape[0] % 1024 == 0
    )
    sketches = piped_sketches if piped else plain_sketches
    reduced, scale, table = sketches(
        verdict_states,
        gate_weight,
        up_weight,
        wvec,
        table,
        sketch_in,
        sketch_out,
        rows,
        length,
    )

    sign = 2.0 * verdict_labels.astype(jnp.float32) - 1.0
    coef = -sign * jax.nn.sigmoid(-sign * reduced[:, width])
    scaled = reduced[:, :width] * (coef * scale)[:, None]
    diff = (scaled - scaled[partner]).astype(jnp.bfloat16)

    mine = rows // parts
    table_high = table.astype(jnp.bfloat16)
    table_low = (table - table_high.astype(jnp.float32)).astype(jnp.bfloat16)
    score_part = lax.dot_general(
        diff, table_high, CONTRACT, preferred_element_type=jnp.float32
    ) + lax.dot_general(diff, table_low, CONTRACT, preferred_element_type=jnp.float32)
    factor = (SOURCES / (store.shape[0] * CORES * lax.axis_size("chip"))) ** 0.5
    scores = sum_scores(score_part * factor, mine)
    contrast_part = lax.dot_general(
        diff, store, CONTRACT, preferred_element_type=jnp.float32
    ).astype(jnp.bfloat16)
    contrast = sum_contrast(contrast_part, mine)
    return (contrast, scores)


def solution(mesh):
    ex, pd = mesh.shape["ex"], mesh.shape["pd"]
    axed = Mesh(mesh.devices.reshape(ex // CORES, CORES, pd), ("chip", "core", "pd"))
    every = ("chip", "core", "pd")
    in_specs = (
        P(every, None),
        P(),
        P(),
        P(None, every),
        P(None, every),
        P(every, None),
        P(),
        P(),
        P(None, every),
        P(("chip", "core"), "pd"),
        P(("chip", "core")),
    )
    out_specs = (P("pd", ("chip", "core")), P("pd", None))
    return jax.shard_map(
        on_device, mesh=axed, in_specs=in_specs, out_specs=out_specs, check_vma=False
    )
```

```python
import functools

import jax
import jax.numpy as jnp
from jax import lax
from jax.experimental import pallas as pl
from jax.experimental.pallas import tpu as pltpu
from jax.sharding import Mesh
from jax.sharding import PartitionSpec as P

SOURCES = 512
CORES = 2
CONTRACT = (((1,), (1,)), ((), ()))


def swap(value, axis, mask):
    size = lax.axis_size(axis)
    return lax.ppermute(value, axis, [(i, i ^ mask) for i in range(size)])


def turn(value, axis, shift):
    size = lax.axis_size(axis)
    return lax.ppermute(value, axis, [(i, (i + shift) % size) for i in range(size)])


def pick(value, index, axis):
    return lax.dynamic_index_in_dim(value, index, axis, keepdims=False)


def source_table(store, source_ids):
    onehot = (source_ids[None, :] == jnp.arange(SOURCES, dtype=jnp.int32)[:, None]).astype(
        jnp.bfloat16
    )
    return jnp.dot(onehot, store, preferred_element_type=jnp.float32)


def reduce_rows(part):
    rows, parts, width = part.shape
    core, pd = lax.axis_index("core"), lax.axis_index("pd")
    halves = part.reshape(CORES, rows // CORES, parts, width)
    half = pick(halves, core, 0) + swap(pick(halves, 1 - core, 0), "core", 1)
    total = pick(half, pd, 1)
    for k in range(1, parts):
        total = total + swap(pick(half, pd ^ k, 1), "pd", k)
    whole = total
    for k in range(1, lax.axis_size("chip")):
        whole = whole + turn(total, "chip", k)
    other = swap(whole, "core", 1)
    first = jnp.where(core == 0, whole, other)
    second = jnp.where(core == 0, other, whole)
    return jnp.concatenate([first, second], axis=0)


def layer_kernel(count, length, *refs):
    pieces = refs[:count]
    gate_w, up_w, sout, wvec, bout, lrow, x, w, acc, sems = refs[count:]
    step = pl.program_id(0)
    steps = pl.num_programs(0)
    block = x.shape[1]
    features = gate_w.shape[1]
    tokens = pieces[0].shape[0]

    def copies(k):
        slot = lax.rem(k, 2)
        here = pl.ds(pl.multiple_of(k * block, block), block)
        return [
            pltpu.make_async_copy(
                weight.at[here, :],
                w.at[slot, :, pl.ds(i * features, features)],
                sems.at[slot, i],
            )
            for i, weight in enumerate((gate_w, up_w))
        ]

    @pl.when(step == 0)
    def _():
        for copy in copies(step):
            copy.start()
        acc[...] = jnp.zeros_like(acc)

    @pl.when(step + 1 < steps)
    def _():
        for copy in copies(step + 1):
            copy.start()

    for i, piece in enumerate(pieces):
        x[i * tokens : (i + 1) * tokens, :] = piece[...]
    for copy in copies(step):
        copy.wait()
    acc[...] += jnp.dot(x[...], w[lax.rem(step, 2)], preferred_element_type=jnp.float32)

    @pl.when(step == steps - 1)
    def _():
        chunk = 64
        groups = length // 8
        rows = chunk // length
        for i in range(acc.shape[0] // chunk):
            here = pl.ds(i * chunk, chunk)
            gate = acc[here, :features]
            weighted = acc[here, features:] * wvec[...]
            sig = jax.nn.sigmoid(gate)
            hidden = gate * sig * weighted
            total = hidden[:, :128]
            for j in range(1, features // 128):
                total = total + hidden[:, j * 128 : (j + 1) * 128]
            total = total.reshape(rows, groups, 8, 128).sum(axis=1)
            lrow[pl.ds(8 * rows * i, 8 * rows), :] = total.reshape(8 * rows, 128)
            dgate = (weighted * sig * (1.0 + gate * (1.0 - sig))).astype(jnp.bfloat16)
            bout[here, :] = lax.dot_general(
                dgate, sout[...], CONTRACT, preferred_element_type=jnp.float32
            )


def layer(pieces, gate_weight, up_weight, sketch_out, wvec, length):
    count = len(pieces)
    tokens, depth = pieces[0].shape
    total = count * tokens
    features = gate_weight.shape[1]
    kout = sketch_out.shape[0]
    rows = total // length
    block = min(2048, depth)
    bout, lrow = pl.pallas_call(
        functools.partial(layer_kernel, count, length),
        grid=(depth // block,),
        in_specs=[pl.BlockSpec((tokens, block), lambda k: (0, k))] * count
        + [
            pl.BlockSpec(memory_space=pl.ANY),
            pl.BlockSpec(memory_space=pl.ANY),
            pl.BlockSpec((kout, features), lambda k: (0, 0)),
            pl.BlockSpec((1, features), lambda k: (0, 0)),
        ],
        out_specs=[
            pl.BlockSpec((total, kout), lambda k: (0, 0)),
            pl.BlockSpec((rows * 8, 128), lambda k: (0, 0)),
        ],
        out_shape=[
            jax.ShapeDtypeStruct((total, kout), jnp.float32),
            jax.ShapeDtypeStruct((rows * 8, 128), jnp.float32),
        ],
        scratch_shapes=[
            pltpu.VMEM((total, block), jnp.bfloat16),
            pltpu.VMEM((2, block, 2 * features), jnp.bfloat16),
            pltpu.VMEM((total, 2 * features), jnp.float32),
            pltpu.SemaphoreType.DMA((2, 2)),
        ],
        compiler_params=pltpu.CompilerParams(vmem_limit_bytes=60 * 1024 * 1024),
        cost_estimate=pl.CostEstimate(
            flops=4 * total * depth * features,
            bytes_accessed=2 * depth * (2 * features + total),
            transcendentals=total * features,
        ),
    )(*pieces, gate_weight, up_weight, sketch_out, wvec)
    return bout.reshape(count, tokens, kout), lrow.reshape(count, -1, 8, 128)


def add_logit(sketch, logit, parts):
    rows = sketch.shape[0]
    wide = jnp.broadcast_to(logit[:, None, None], (rows, parts, 128))
    return jnp.concatenate([sketch.reshape(rows, parts, -1), wide], axis=2)


def sibling(value):
    return swap(value, "core", 1)


def plane_perm(masks):
    parts = lax.axis_size("pd")
    return [
        (core * parts + pd, core * parts + (pd ^ masks[core]))
        for core in range(CORES)
        for pd in range(parts)
    ]


def plane_sum(part):
    core, pd = lax.axis_index("core"), lax.axis_index("pd")
    half = pick(part, core, 1) + sibling(pick(part, 1 - core, 1))
    total = pick(half, pd, 2)
    for k in range(1, part.shape[3]):
        total = total + swap(pick(half, pd ^ k, 2), "pd", k)
    return total


def piped_sketches(
    states, gate_weight, up_weight, wvec, table, sketch_in, sketch_out, rows, length
):
    parts, chips = lax.axis_size("pd"), lax.axis_size("chip")
    place, core, pd = lax.axis_index("chip"), lax.axis_index("core"), lax.axis_index("pd")
    mine = states.shape[0]
    kin, kout = sketch_in.shape[0], sketch_out.shape[0]
    first, second = (2, 1), (1, 2)
    plane = ("core", "pd")
    tie = lax.optimization_barrier

    def send_a(value):
        return lax.ppermute(value, plane, plane_perm(first))

    def send_b(value):
        return lax.ppermute(value, plane, plane_perm(second))

    def run(*pieces):
        return layer(pieces, gate_weight, up_weight, sketch_out, wvec, length)

    cores = jnp.arange(CORES)[:, None]
    apart = jnp.arange(parts)[None, :] ^ pd
    is_a = jnp.where(cores == 0, apart == first[0], apart == first[1])
    base = jnp.where(apart == 0, 0, jnp.where(apart == 3, 6, jnp.where(is_a, 2, 4)))
    slot = (base + (cores != core)).reshape(-1)

    def sketch_of(bout, lrow, layer_index):
        logit = lrow.reshape(len(slot), mine // length, -1).sum(axis=2)[slot]
        sketch = jnp.einsum(
            "rti,rto->rio",
            pick(ain, layer_index, 0).reshape(-1, length, kin),
            bout[slot].reshape(-1, length, kout),
            precision=lax.Precision.HIGHEST,
        ).reshape(-1, kin * kout)
        part = add_logit(sketch, logit.reshape(-1), parts)
        return part.reshape(CORES, -1, *part.shape[1:])

    own = states
    a, b, later = send_a(own), send_b(own), turn(own, "chip", 1)
    own_s = sibling(own)
    ain = lax.dot_general(states, sketch_in, CONTRACT, preferred_element_type=jnp.float32)
    ain = lax.all_gather(ain, ("chip", "core", "pd"), axis=0, tiled=True)
    ain = ain.reshape(chips, -1, kin)
    a, b, table, wvec = tie((a, b, table, wvec))
    total_table = lax.psum(table, ("chip", "core"))
    held, outs, sums = [], [], []
    for step in range(chips):
        last = step == chips - 1
        a_s, b_s = sibling(a), (None if last else sibling(b))
        d = send_b(a)
        pieces = held + [own, own_s, a, a_s] + ([] if last else [b, b_s])
        if not last:
            own = later
            own_s = sibling(own)
            next_a, next_b = send_a(own), send_b(own)
            if step < chips - 2:
                later = turn(own, "chip", 1)
        outs.append(run(*pieces))
        if last:
            early = plane_sum(jnp.stack(sums))
            early = [early] + [turn(early, "chip", k) for k in range(1, chips)]
            b, d, outs[-1], early = tie((b, d, outs[-1], early))
            outs.append(run(b, sibling(b), d, sibling(d)))
        elif step < chips - 2:
            d, a, b, later, outs[-1] = tie((d, next_a, next_b, later, outs[-1]))
            held = [d, sibling(d)]
        else:
            d, a, outs[-1] = tie((d, next_a, outs[-1]))
            b = next_b
            held = [d, sibling(d)]
        if 1 <= step < chips - 1:
            low, high = outs[step - 1], outs[step]
            skip = 0 if step == 1 else 2
            bout, lrow = (jnp.concatenate([p[skip:], q[:2]]) for p, q in zip(low, high))
            sums.append(sketch_of(bout, lrow, (place - step + 1) % chips))
    late = []
    for r in (chips - 2, chips - 1):
        parts_of = [o for o in outs[r : r + 2]]
        if r == chips - 2:
            bout, lrow = (jnp.concatenate([p[2:], q[:2]]) for p, q in zip(*parts_of))
        else:
            bout, lrow = (jnp.concatenate([p[2:], q]) for p, q in zip(*parts_of))
        late.append(sketch_of(bout, lrow, (place - r) % chips))
    late = plane_sum(jnp.stack(late))
    late = [late] + [turn(late, "chip", k) for k in range(1, chips)]
    cut = chips - 2
    whole = []
    for j in range(chips):
        rounds = [(k, (j - k) % chips) for k in range(chips)]
        whole.append(sum(early[k][r] if r < cut else late[k][r - cut] for k, r in rounds))
    whole = jnp.stack(whole)
    both = jnp.stack([whole, sibling(whole)])
    per = both.shape[2]
    row = jnp.arange(rows)
    at_layer, at_core, at = row // (CORES * per), row // per % CORES, row % per
    index = ((at_core != core) * chips + (place - at_layer) % chips) * per + at
    return both.reshape(rows, -1)[index], total_table


def contrast_kernel(blocks, diff, store, table, *outs):
    step = pl.program_id(0)
    mine = outs[0].shape[0]

    @pl.when(step < blocks)
    def _():
        part = lax.dot_general(diff[...], store[...], CONTRACT, preferred_element_type=jnp.float32)
        for i, out in enumerate(outs):
            out[...] = part[i * mine : (i + 1) * mine].astype(out.dtype)

    @pl.when(step == blocks)
    def _():
        both = lax.dot_general(diff[...], table[...], CONTRACT, preferred_element_type=jnp.float32)
        half = both.shape[1] // 2
        score = both[:, :half] + both[:, half:]
        high = score.astype(jnp.bfloat16)
        low = (score - high.astype(jnp.float32)).astype(jnp.bfloat16)
        for i, out in enumerate(outs):
            out[:, :half] = high[i * mine : (i + 1) * mine]
            out[:, half:] = low[i * mine : (i + 1) * mine]


def contrast_parts(diff, store, table, parts):
    rows, width = diff.shape
    examples = store.shape[0]
    block = table.shape[0]
    blocks = examples // block
    mine = rows // parts
    return pl.pallas_call(
        functools.partial(contrast_kernel, blocks),
        grid=(blocks + 1,),
        in_specs=[
            pl.BlockSpec((rows, width), lambda k: (0, 0)),
            pl.BlockSpec((block, width), lambda k: (jnp.minimum(k, blocks - 1), 0)),
            pl.BlockSpec((block, width), lambda k: (0, 0)),
        ],
        out_specs=[pl.BlockSpec((mine, block), lambda k: (0, k))] * parts,
        out_shape=[jax.ShapeDtypeStruct((mine, examples + block), jnp.bfloat16)] * parts,
        compiler_params=pltpu.CompilerParams(vmem_limit_bytes=60 * 1024 * 1024),
        cost_estimate=pl.CostEstimate(
            flops=2 * rows * width * (examples + block),
            bytes_accessed=2 * width * (examples + block) + 2 * rows * (examples + block),
            transcendentals=0,
        ),
    )(diff, store, table)


def plain_sketches(
    states, gate_weight, up_weight, wvec, table, sketch_in, sketch_out, rows, length
):
    kin, kout = sketch_in.shape[0], sketch_out.shape[0]
    ff_local = gate_weight.shape[1]
    states = lax.all_gather(states, ("chip", "core", "pd"), axis=0, tiled=True)
    gate = jnp.dot(states, gate_weight, preferred_element_type=jnp.float32)
    up = jnp.dot(states, up_weight, preferred_element_type=jnp.float32)
    ain = lax.dot_general(states, sketch_in, CONTRACT, preferred_element_type=jnp.float32)
    sig = jax.nn.sigmoid(gate)
    weighted = up * wvec
    logit = jnp.sum((gate * sig * weighted).reshape(rows, length * ff_local), axis=1)
    dgate = (weighted * sig * (1.0 + gate * (1.0 - sig))).astype(jnp.bfloat16)
    bout = lax.dot_general(dgate, sketch_out, CONTRACT, preferred_element_type=jnp.float32)
    sketch = jnp.einsum(
        "rti,rto->rio",
        ain.reshape(rows, length, kin),
        bout.reshape(rows, length, kout),
        precision=lax.Precision.HIGHEST,
    ).reshape(rows, kin * kout)
    return reduce_rows(add_logit(sketch, logit, lax.axis_size("pd"))), lax.psum(table, ("chip", "core"))


def on_device(
    verdict_states,
    verdict_labels,
    partner,
    gate_weight,
    up_weight,
    down_weight,
    readout,
    sketch_in,
    sketch_out,
    store,
    source_ids,
):
    rows = verdict_labels.shape[0]
    parts, chips = lax.axis_size("pd"), lax.axis_size("chip")
    pd = lax.axis_index("pd")
    examples, width = store.shape
    mine = verdict_states.shape[0]
    length = mine * parts * CORES * chips // rows

    wvec = jnp.dot(down_weight, readout, preferred_element_type=jnp.float32)[None, :]
    table = source_table(store, source_ids)
    piped = (
        parts == 4
        and chips == 4
        and mine == 2 * length
        and length == 32
        and gate_weight.shape[1] % 128 == 0
        and gate_weight.shape[0] % 2048 == 0
    )
    sketches = piped_sketches if piped else plain_sketches
    reduced, table = sketches(
        verdict_states,
        gate_weight,
        up_weight,
        wvec,
        table,
        sketch_in,
        sketch_out,
        rows,
        length,
    )

    sign = 2.0 * verdict_labels.astype(jnp.float32) - 1.0
    coef = -sign * jax.nn.sigmoid(-sign * (reduced[:, width] / length))
    scaled = reduced[:, :width] * (coef / length)[:, None]
    group = rows // parts
    order = jnp.concatenate([(pd ^ k) * group + jnp.arange(group) for k in range(parts)])
    diff = (scaled[order] - scaled[partner[order]]).astype(jnp.bfloat16)

    table_high = table.astype(jnp.bfloat16)
    table_low = (table - table_high.astype(jnp.float32)).astype(jnp.bfloat16)
    blocks = contrast_parts(diff, store, jnp.concatenate([table_high, table_low]), parts)
    total = blocks[0].astype(jnp.float32)
    for k in range(1, parts):
        total = total + swap(blocks[k], "pd", k).astype(jnp.float32)
    factor = (SOURCES / (examples * CORES * chips)) ** 0.5
    scores = total[:, examples : examples + SOURCES] + total[:, examples + SOURCES :]
    return (total[:, :examples], scores * factor)


def solution(mesh):
    ex, pd = mesh.shape["ex"], mesh.shape["pd"]
    axed = Mesh(mesh.devices.reshape(ex // CORES, CORES, pd), ("chip", "core", "pd"))
    every = ("chip", "core", "pd")
    in_specs = (
        P(every, None),
        P(),
        P(),
        P(None, every),
        P(None, every),
        P(every, None),
        P(),
        P(),
        P(None, every),
        P(("chip", "core"), "pd"),
        P(("chip", "core")),
    )
    out_specs = (P("pd", ("chip", "core")), P("pd", None))
    return jax.shard_map(
        on_device, mesh=axed, in_specs=in_specs, out_specs=out_specs, check_vma=False
    )
```

```python
import functools

import jax
import jax.numpy as jnp
from jax import lax
from jax.experimental import pallas as pl
from jax.experimental.pallas import tpu as pltpu
from jax.sharding import Mesh
from jax.sharding import PartitionSpec as P

SOURCES = 512
CORES = 2
CONTRACT = (((1,), (1,)), ((), ()))


def swap(value, axis, mask):
    size = lax.axis_size(axis)
    return lax.ppermute(value, axis, [(i, i ^ mask) for i in range(size)])


def turn(value, axis, shift):
    size = lax.axis_size(axis)
    return lax.ppermute(value, axis, [(i, (i + shift) % size) for i in range(size)])


def pick(value, index, axis):
    return lax.dynamic_index_in_dim(value, index, axis, keepdims=False)


def reduce_rows(part):
    rows, parts, width = part.shape
    core, pd = lax.axis_index("core"), lax.axis_index("pd")
    halves = part.reshape(CORES, rows // CORES, parts, width)
    half = pick(halves, core, 0) + swap(pick(halves, 1 - core, 0), "core", 1)
    total = pick(half, pd, 1)
    for k in range(1, parts):
        total = total + swap(pick(half, pd ^ k, 1), "pd", k)
    whole = total
    for k in range(1, lax.axis_size("chip")):
        whole = whole + turn(total, "chip", k)
    other = swap(whole, "core", 1)
    first = jnp.where(core == 0, whole, other)
    second = jnp.where(core == 0, other, whole)
    return jnp.concatenate([first, second], axis=0)


def layer_kernel(count, length, *refs):
    pieces = refs[:count]
    gate_w, up_w, sin, sout, wvec, proj, lrow, x, w, acc, dgate, sems = refs[count:]
    step = pl.program_id(0)
    steps = pl.num_programs(0)
    block = x.shape[1]
    features = gate_w.shape[1]
    tokens = pieces[0].shape[0]
    kin = sin.shape[0]

    def copies(k):
        slot = lax.rem(k, 2)
        here = pl.ds(pl.multiple_of(k * block, block), block)
        return [
            pltpu.make_async_copy(
                weight.at[here, :],
                w.at[slot, :, pl.ds(i * features, features)],
                sems.at[slot, i],
            )
            for i, weight in enumerate((gate_w, up_w))
        ]

    @pl.when(step == 0)
    def _():
        for copy in copies(step):
            copy.start()
        acc[...] = jnp.zeros_like(acc)
        proj[...] = jnp.zeros_like(proj)

    @pl.when(step + 1 < steps)
    def _():
        for copy in copies(step + 1):
            copy.start()

    for i, piece in enumerate(pieces):
        x[i * tokens : (i + 1) * tokens, :] = piece[...]
    for copy in copies(step):
        copy.wait()
    proj[:, :kin] += lax.dot_general(x[...], sin[...], CONTRACT, preferred_element_type=jnp.float32)
    acc[...] += jnp.dot(x[...], w[lax.rem(step, 2)], preferred_element_type=jnp.float32)

    @pl.when(step == steps - 1)
    def _():
        @pl.loop(0, acc.shape[0] // length)
        def _(i):
            here = pl.ds(pl.multiple_of(i * length, length), length)
            total = jnp.zeros((length, 128), jnp.float32)
            for j in range(features // 128):
                at = slice(j * 128, (j + 1) * 128)
                gate = acc[here, at]
                weighted = acc[here, features + j * 128 : features + (j + 1) * 128] * wvec[:, at]
                sig = jax.nn.sigmoid(gate)
                swish = gate * sig
                total = total + swish * weighted
                dgate[here, at] = (weighted * (sig + swish * (1.0 - sig))).astype(jnp.bfloat16)
            lrow[pl.ds(pl.multiple_of(8 * i, 8), 8), :] = total.reshape(-1, 8, 128).sum(axis=0)

        proj[:, kin:] = lax.dot_general(
            dgate[...], sout[...], CONTRACT, preferred_element_type=jnp.float32
        )


def layer(pieces, gate_weight, up_weight, sketch_in, sketch_out, wvec, length):
    count = len(pieces)
    tokens, depth = pieces[0].shape
    total = count * tokens
    features = gate_weight.shape[1]
    kin, kout = sketch_in.shape[0], sketch_out.shape[0]
    rows = total // length
    block = min(1024, depth)
    return pl.pallas_call(
        functools.partial(layer_kernel, count, length),
        grid=(depth // block,),
        in_specs=[pl.BlockSpec((tokens, block), lambda k: (0, k))] * count
        + [
            pl.BlockSpec(memory_space=pl.ANY),
            pl.BlockSpec(memory_space=pl.ANY),
            pl.BlockSpec((kin, block), lambda k: (0, k)),
            pl.BlockSpec((kout, features), lambda k: (0, 0)),
            pl.BlockSpec((1, features), lambda k: (0, 0)),
        ],
        out_specs=[
            pl.BlockSpec((total, kin + kout), lambda k: (0, 0)),
            pl.BlockSpec((rows * 8, 128), lambda k: (0, 0)),
        ],
        out_shape=[
            jax.ShapeDtypeStruct((total, kin + kout), jnp.float32),
            jax.ShapeDtypeStruct((rows * 8, 128), jnp.float32),
        ],
        scratch_shapes=[
            pltpu.VMEM((total, block), jnp.bfloat16),
            pltpu.VMEM((2, block, 2 * features), jnp.bfloat16),
            pltpu.VMEM((total, 2 * features), jnp.float32),
            pltpu.VMEM((total, features), jnp.bfloat16),
            pltpu.SemaphoreType.DMA((2, 2)),
        ],
        compiler_params=pltpu.CompilerParams(vmem_limit_bytes=60 * 1024 * 1024),
        cost_estimate=pl.CostEstimate(
            flops=4 * total * depth * features,
            bytes_accessed=2 * depth * (2 * features + total),
            transcendentals=total * features,
        ),
    )(*pieces, gate_weight, up_weight, sketch_in, sketch_out, wvec)


def table_kernel(ids, store, out, acc):
    step = pl.program_id(0)

    @pl.when(step == 0)
    def _():
        acc[...] = jnp.zeros_like(acc)

    labels = lax.broadcasted_iota(jnp.int32, (acc.shape[0], store.shape[0]), 0)
    onehot = jnp.where(labels == ids[...], 1.0, 0.0).astype(jnp.bfloat16)
    acc[...] += jnp.dot(onehot, store[...], preferred_element_type=jnp.float32)

    @pl.when(step == pl.num_programs(0) - 1)
    def _():
        sources = acc.shape[0]
        high = acc[...].astype(jnp.bfloat16)
        out[:sources, :] = high
        out[sources:, :] = (acc[...] - high.astype(jnp.float32)).astype(jnp.bfloat16)


def source_table(store, source_ids):
    examples, width = store.shape
    block = 1024
    return pl.pallas_call(
        table_kernel,
        grid=(examples // block,),
        in_specs=[
            pl.BlockSpec((1, block), lambda k: (0, k)),
            pl.BlockSpec((block, width), lambda k: (k, 0)),
        ],
        out_specs=pl.BlockSpec((2 * SOURCES, width), lambda k: (0, 0)),
        out_shape=jax.ShapeDtypeStruct((2 * SOURCES, width), jnp.bfloat16),
        scratch_shapes=[pltpu.VMEM((SOURCES, width), jnp.float32)],
        compiler_params=pltpu.CompilerParams(vmem_limit_bytes=60 * 1024 * 1024),
        cost_estimate=pl.CostEstimate(
            flops=2 * SOURCES * examples * width,
            bytes_accessed=2 * examples * width,
            transcendentals=0,
        ),
    )(source_ids.reshape(1, -1), store)


def add_logit(sketch, logit, parts):
    rows = sketch.shape[0]
    wide = jnp.broadcast_to(logit[:, None, None], (rows, parts, 128))
    return jnp.concatenate([sketch.reshape(rows, parts, -1), wide], axis=2)


def sibling(value):
    return swap(value, "core", 1)


def plane_perm(masks):
    parts = lax.axis_size("pd")
    return [
        (core * parts + pd, core * parts + (pd ^ masks[core]))
        for core in range(CORES)
        for pd in range(parts)
    ]


def piped_sketches(
    states, gate_weight, up_weight, wvec, table, sketch_in, sketch_out, rows, length
):
    parts, chips = lax.axis_size("pd"), lax.axis_size("chip")
    place, core, pd = lax.axis_index("chip"), lax.axis_index("core"), lax.axis_index("pd")
    mine = states.shape[0]
    kin, kout = sketch_in.shape[0], sketch_out.shape[0]
    first, second = (2, 1), (1, 2)
    plane = ("core", "pd")
    tie = lax.optimization_barrier

    def send_a(value):
        return lax.ppermute(value, plane, plane_perm(first))

    def send_b(value):
        return lax.ppermute(value, plane, plane_perm(second))

    def ring(value, shift=1):
        return turn(value, "chip", shift)

    sin = sketch_in.reshape(parts, kin // parts, -1)[jnp.arange(parts) ^ pd]
    sin = sin.reshape(sketch_in.shape)

    def run(*pieces):
        return layer(pieces, gate_weight, up_weight, sin, sketch_out, wvec, length)

    p0 = states
    p0s = sibling(p0)
    a0, b0, p1 = send_a(p0), send_b(p0), ring(p0)
    a0, b0, table, wvec, sin = tie((a0, b0, table, wvec, sin))
    a0s, b0s = sibling(a0), sibling(b0)
    d0 = send_b(a0)
    a1, b1, p2 = send_a(p1), send_b(p1), ring(p1)
    out0 = run(p0, p0s, a0, a0s, b0, b0s)
    p1s = sibling(p1)
    a1, b1, d0, p2, out0 = tie((a1, b1, d0, p2, out0))
    a1s, b1s, d0s = sibling(a1), sibling(b1), sibling(d0)
    d1 = ring(d0)
    a2, b2, p3 = send_a(p2), send_b(p2), ring(p2)
    out1 = run(d0, d0s, p1, p1s, a1, a1s, b1, b1s)
    p2s = sibling(p2)
    a2, b2, d1, p3, out1 = tie((a2, b2, d1, p3, out1))
    a2s, b2s, d1s = sibling(a2), sibling(b2), sibling(d1)
    d2, d3 = ring(d1), ring(d0, -1)
    a3, b3 = send_a(p3), send_b(p3)
    out2 = run(d1, d1s, p2, p2s, a2, a2s, b2, b2s)
    p3s = sibling(p3)
    a3, b3, d2, d3, out2 = tie((a3, b3, d2, d3, out2))
    out3 = run(
        d2, sibling(d2), p3, p3s, a3, sibling(a3), b3, sibling(b3), d3, sibling(d3)
    )
    outs = (out0, out1, out2, out3)

    cores = (core + jnp.arange(CORES)) % CORES
    apart = jnp.arange(parts)[None, :] ^ pd
    is_a = jnp.where(cores[:, None] == 0, apart == first[0], apart == first[1])
    slot = jnp.where(apart == 0, 0, jnp.where(apart == 3, 6, jnp.where(is_a, 2, 4)))
    slot = slot + jnp.arange(CORES)[:, None]
    order = slot[:, None, :] + 2 * parts * jnp.arange(chips)[None, :, None]
    order = order.reshape(-1)
    pieces = order.shape[0]
    proj = jnp.concatenate([o[0] for o in outs]).reshape(pieces, -1, kin + kout)[order]
    logit = jnp.concatenate([o[1] for o in outs]).reshape(pieces, -1, 8 * 128).sum(axis=2)[order]
    proj = proj.reshape(rows, length, kin + kout)
    sketch = jnp.einsum(
        "rti,rto->rio", proj[:, :, :kin], proj[:, :, kin:], precision=lax.Precision.HIGHEST
    )
    part = add_logit(sketch.reshape(rows, kin * kout), logit.reshape(rows), parts)
    half = part[: rows // CORES] + sibling(part[rows // CORES :])
    total = half[:, 0]
    for k in range(1, parts):
        total = total + swap(half[:, k], "pd", k)
    total = total.reshape(chips, -1, total.shape[1])
    got = [total] + [ring(total, k) for k in range(1, chips)]
    whole = jnp.stack([sum(got[k][(j - k) % chips] for k in range(chips)) for j in range(chips)])
    per = whole.shape[1]
    both = jnp.concatenate([whole, sibling(whole)]).reshape(rows, -1)
    row = jnp.arange(rows)
    at_layer, at_core, at = row // (CORES * per), row // per % CORES, row % per
    index = ((at_core != core) * chips + (place - at_layer) % chips) * per + at
    return both, index, table


def contrast_kernel(with_table, diff, *refs):
    step = pl.program_id(0)
    lead = 1 if with_table else 0
    table, store, outs = (refs[0], refs[1], refs[2:]) if with_table else (None, refs[0], refs[1:])
    mine = outs[0].shape[0]

    if with_table:

        @pl.when(step == 0)
        def _():
            both = lax.dot_general(
                diff[...], table[...], CONTRACT, preferred_element_type=jnp.float32
            )
            half = both.shape[1] // 2
            score = both[:, :half] + both[:, half:]
            high = score.astype(jnp.bfloat16)
            low = (score - high.astype(jnp.float32)).astype(jnp.bfloat16)
            for i, out in enumerate(outs):
                out[:, :half] = high[i * mine : (i + 1) * mine]
                out[:, half:] = low[i * mine : (i + 1) * mine]

    @pl.when(step >= lead)
    def _():
        part = lax.dot_general(diff[...], store[...], CONTRACT, preferred_element_type=jnp.float32)
        for i, out in enumerate(outs):
            out[...] = part[i * mine : (i + 1) * mine].astype(out.dtype)


def contrast_parts(diff, store, first, blocks, parts, table=None):
    rows, width = diff.shape
    block = 2 * SOURCES
    lead = 0 if table is None else 1
    mine = rows // parts
    columns = block * (blocks + lead)
    tables = [] if table is None else [table]
    return pl.pallas_call(
        functools.partial(contrast_kernel, table is not None),
        grid=(blocks + lead,),
        in_specs=[pl.BlockSpec((rows, width), lambda k: (0, 0))]
        + [pl.BlockSpec((block, width), lambda k: (0, 0))] * lead
        + [pl.BlockSpec((block, width), lambda k: (first + jnp.maximum(k - lead, 0), 0))],
        out_specs=[pl.BlockSpec((mine, block), lambda k: (0, k))] * parts,
        out_shape=[jax.ShapeDtypeStruct((mine, columns), jnp.bfloat16)] * parts,
        compiler_params=pltpu.CompilerParams(vmem_limit_bytes=60 * 1024 * 1024),
        cost_estimate=pl.CostEstimate(
            flops=2 * rows * width * columns,
            bytes_accessed=2 * (width + rows) * columns,
            transcendentals=0,
        ),
    )(diff, *tables, store)


def exchange(blocks):
    total = blocks[0].astype(jnp.float32)
    for k in range(1, len(blocks)):
        total = total + swap(blocks[k], "pd", k).astype(jnp.float32)
    return total


def plain_sketches(
    states, gate_weight, up_weight, wvec, table, sketch_in, sketch_out, rows, length
):
    kin, kout = sketch_in.shape[0], sketch_out.shape[0]
    ff_local = gate_weight.shape[1]
    states = lax.all_gather(states, ("chip", "core", "pd"), axis=0, tiled=True)
    gate = jnp.dot(states, gate_weight, preferred_element_type=jnp.float32)
    up = jnp.dot(states, up_weight, preferred_element_type=jnp.float32)
    ain = lax.dot_general(states, sketch_in, CONTRACT, preferred_element_type=jnp.float32)
    sig = jax.nn.sigmoid(gate)
    weighted = up * wvec
    logit = jnp.sum((gate * sig * weighted).reshape(rows, length * ff_local), axis=1)
    dgate = (weighted * sig * (1.0 + gate * (1.0 - sig))).astype(jnp.bfloat16)
    bout = lax.dot_general(dgate, sketch_out, CONTRACT, preferred_element_type=jnp.float32)
    sketch = jnp.einsum(
        "rti,rto->rio",
        ain.reshape(rows, length, kin),
        bout.reshape(rows, length, kout),
        precision=lax.Precision.HIGHEST,
    ).reshape(rows, kin * kout)
    reduced = reduce_rows(add_logit(sketch, logit, lax.axis_size("pd")))
    return reduced, jnp.arange(rows), table


def on_device(
    verdict_states,
    verdict_labels,
    partner,
    gate_weight,
    up_weight,
    down_weight,
    readout,
    sketch_in,
    sketch_out,
    store,
    source_ids,
):
    rows = verdict_labels.shape[0]
    parts, chips = lax.axis_size("pd"), lax.axis_size("chip")
    pd = lax.axis_index("pd")
    examples, width = store.shape
    mine = verdict_states.shape[0]
    length = mine * parts * CORES * chips // rows

    wvec = jnp.dot(down_weight, readout, preferred_element_type=jnp.float32)[None, :]
    table = source_table(store, source_ids)
    piped = (
        parts == 4
        and chips == 4
        and mine == 2 * length
        and length == 32
        and gate_weight.shape[1] % 128 == 0
        and gate_weight.shape[0] % 1024 == 0
    )
    sketches = piped_sketches if piped else plain_sketches
    reduced, index, table = sketches(
        verdict_states,
        gate_weight,
        up_weight,
        wvec,
        table,
        sketch_in,
        sketch_out,
        rows,
        length,
    )

    labels = jnp.zeros_like(verdict_labels).at[index].set(verdict_labels)
    sign = 2.0 * labels.astype(jnp.float32) - 1.0
    coef = -sign * jax.nn.sigmoid(-sign * (reduced[:, width] / length))
    scaled = reduced[:, :width] * (coef / length)[:, None]
    group = rows // parts
    order = jnp.concatenate([(pd ^ k) * group + jnp.arange(group) for k in range(parts)])
    diff = (scaled[index[order]] - scaled[index[partner[order]]]).astype(jnp.bfloat16)

    blocks = examples // (2 * SOURCES)
    early = blocks // 2
    front = exchange(contrast_parts(diff, store, 0, early, parts, table))
    back = exchange(contrast_parts(diff, store, early, blocks - early, parts))
    scores = front[:, :SOURCES] + front[:, SOURCES : 2 * SOURCES]
    whole = scores
    for k in range(1, chips):
        whole = whole + turn(scores, "chip", k)
    whole = whole + sibling(whole)
    factor = (SOURCES / (examples * CORES * chips)) ** 0.5
    contrast = jnp.concatenate([front[:, 2 * SOURCES :], back], axis=1)
    return (contrast, whole * factor)


def solution(mesh):
    ex, pd = mesh.shape["ex"], mesh.shape["pd"]
    axed = Mesh(mesh.devices.reshape(ex // CORES, CORES, pd), ("chip", "core", "pd"))
    every = ("chip", "core", "pd")
    in_specs = (
        P(every, None),
        P(),
        P(),
        P(None, every),
        P(None, every),
        P(every, None),
        P(),
        P(),
        P(None, every),
        P(("chip", "core"), "pd"),
        P(("chip", "core")),
    )
    out_specs = (P("pd", ("chip", "core")), P("pd", None))
    return jax.shard_map(
        on_device, mesh=axed, in_specs=in_specs, out_specs=out_specs, check_vma=False
    )
```

```python
import functools

import jax
import jax.numpy as jnp
from jax import lax
from jax.experimental import pallas as pl
from jax.experimental.pallas import tpu as pltpu
from jax.sharding import Mesh
from jax.sharding import PartitionSpec as P

SOURCES = 512
CORES = 2
CONTRACT = (((1,), (1,)), ((), ()))


def swap(value, axis, mask):
    size = lax.axis_size(axis)
    return lax.ppermute(value, axis, [(i, i ^ mask) for i in range(size)])


def turn(value, axis, shift):
    size = lax.axis_size(axis)
    return lax.ppermute(value, axis, [(i, (i + shift) % size) for i in range(size)])


def pick(value, index, axis):
    return lax.dynamic_index_in_dim(value, index, axis, keepdims=False)


def reduce_rows(part):
    rows, parts, width = part.shape
    core, pd = lax.axis_index("core"), lax.axis_index("pd")
    halves = part.reshape(CORES, rows // CORES, parts, width)
    half = pick(halves, core, 0) + swap(pick(halves, 1 - core, 0), "core", 1)
    total = pick(half, pd, 1)
    for k in range(1, parts):
        total = total + swap(pick(half, pd ^ k, 1), "pd", k)
    whole = total
    for k in range(1, lax.axis_size("chip")):
        whole = whole + turn(total, "chip", k)
    other = swap(whole, "core", 1)
    first = jnp.where(core == 0, whole, other)
    second = jnp.where(core == 0, other, whole)
    return jnp.concatenate([first, second], axis=0)


def layer_kernel(count, length, *refs):
    pieces = refs[:count]
    gate_w, up_w, sin, sout, wvec, proj, lrow, x, w, acc, dgate, sems = refs[count:]
    step = pl.program_id(0)
    steps = pl.num_programs(0)
    block = x.shape[1]
    features = gate_w.shape[1]
    tokens = pieces[0].shape[0]
    kin = sin.shape[0]

    def copies(k):
        slot = lax.rem(k, 2)
        here = pl.ds(pl.multiple_of(k * block, block), block)
        return [
            pltpu.make_async_copy(
                weight.at[here, :],
                w.at[slot, :, pl.ds(i * features, features)],
                sems.at[slot, i],
            )
            for i, weight in enumerate((gate_w, up_w))
        ]

    @pl.when(step == 0)
    def _():
        for copy in copies(step):
            copy.start()
        acc[...] = jnp.zeros_like(acc)
        proj[...] = jnp.zeros_like(proj)

    @pl.when(step + 1 < steps)
    def _():
        for copy in copies(step + 1):
            copy.start()

    for i, piece in enumerate(pieces):
        x[i * tokens : (i + 1) * tokens, :] = piece[...]
    for copy in copies(step):
        copy.wait()
    proj[:, :kin] += lax.dot_general(x[...], sin[...], CONTRACT, preferred_element_type=jnp.float32)
    acc[...] += jnp.dot(x[...], w[lax.rem(step, 2)], preferred_element_type=jnp.float32)

    @pl.when(step == steps - 1)
    def _():
        @pl.loop(0, acc.shape[0] // length)
        def _(i):
            here = pl.ds(pl.multiple_of(i * length, length), length)
            total = jnp.zeros((length, 128), jnp.float32)
            for j in range(features // 128):
                at = slice(j * 128, (j + 1) * 128)
                gate = acc[here, at]
                weighted = acc[here, features + j * 128 : features + (j + 1) * 128] * wvec[:, at]
                sig = jax.nn.sigmoid(gate)
                swish = gate * sig
                total = total + swish * weighted
                dgate[here, at] = (weighted * (sig + swish * (1.0 - sig))).astype(jnp.bfloat16)
            lrow[pl.ds(pl.multiple_of(8 * i, 8), 8), :] = total.reshape(-1, 8, 128).sum(axis=0)

        proj[:, kin:] = lax.dot_general(
            dgate[...], sout[...], CONTRACT, preferred_element_type=jnp.float32
        )


def layer(pieces, gate_weight, up_weight, sketch_in, sketch_out, wvec, length):
    count = len(pieces)
    tokens, depth = pieces[0].shape
    total = count * tokens
    features = gate_weight.shape[1]
    kin, kout = sketch_in.shape[0], sketch_out.shape[0]
    rows = total // length
    block = min(1024, depth)
    return pl.pallas_call(
        functools.partial(layer_kernel, count, length),
        grid=(depth // block,),
        in_specs=[pl.BlockSpec((tokens, block), lambda k: (0, k))] * count
        + [
            pl.BlockSpec(memory_space=pl.ANY),
            pl.BlockSpec(memory_space=pl.ANY),
            pl.BlockSpec((kin, block), lambda k: (0, k)),
            pl.BlockSpec((kout, features), lambda k: (0, 0)),
            pl.BlockSpec((1, features), lambda k: (0, 0)),
        ],
        out_specs=[
            pl.BlockSpec((total, kin + kout), lambda k: (0, 0)),
            pl.BlockSpec((rows * 8, 128), lambda k: (0, 0)),
        ],
        out_shape=[
            jax.ShapeDtypeStruct((total, kin + kout), jnp.float32),
            jax.ShapeDtypeStruct((rows * 8, 128), jnp.float32),
        ],
        scratch_shapes=[
            pltpu.VMEM((total, block), jnp.bfloat16),
            pltpu.VMEM((2, block, 2 * features), jnp.bfloat16),
            pltpu.VMEM((total, 2 * features), jnp.float32),
            pltpu.VMEM((total, features), jnp.bfloat16),
            pltpu.SemaphoreType.DMA((2, 2)),
        ],
        compiler_params=pltpu.CompilerParams(vmem_limit_bytes=60 * 1024 * 1024),
        cost_estimate=pl.CostEstimate(
            flops=4 * total * depth * features,
            bytes_accessed=2 * depth * (2 * features + total),
            transcendentals=total * features,
        ),
    )(*pieces, gate_weight, up_weight, sketch_in, sketch_out, wvec)


def table_kernel(ids, store, out, acc):
    step = pl.program_id(0)

    @pl.when(step == 0)
    def _():
        acc[...] = jnp.zeros_like(acc)

    labels = lax.broadcasted_iota(jnp.int32, (acc.shape[0], store.shape[0]), 0)
    onehot = jnp.where(labels == ids[...], 1.0, 0.0).astype(jnp.bfloat16)
    acc[...] += jnp.dot(onehot, store[...], preferred_element_type=jnp.float32)

    @pl.when(step == pl.num_programs(0) - 1)
    def _():
        sources = acc.shape[0]
        high = acc[...].astype(jnp.bfloat16)
        out[:sources, :] = high
        out[sources:, :] = (acc[...] - high.astype(jnp.float32)).astype(jnp.bfloat16)


def source_table(store, source_ids):
    examples, width = store.shape
    block = 1024
    return pl.pallas_call(
        table_kernel,
        grid=(examples // block,),
        in_specs=[
            pl.BlockSpec((1, block), lambda k: (0, k)),
            pl.BlockSpec((block, width), lambda k: (k, 0)),
        ],
        out_specs=pl.BlockSpec((2 * SOURCES, width), lambda k: (0, 0)),
        out_shape=jax.ShapeDtypeStruct((2 * SOURCES, width), jnp.bfloat16),
        scratch_shapes=[pltpu.VMEM((SOURCES, width), jnp.float32)],
        compiler_params=pltpu.CompilerParams(vmem_limit_bytes=60 * 1024 * 1024),
        cost_estimate=pl.CostEstimate(
            flops=2 * SOURCES * examples * width,
            bytes_accessed=2 * examples * width,
            transcendentals=0,
        ),
    )(source_ids.reshape(1, -1), store)


def add_logit(sketch, logit, parts):
    rows = sketch.shape[0]
    wide = jnp.broadcast_to(logit[:, None, None], (rows, parts, 128))
    return jnp.concatenate([sketch.reshape(rows, parts, -1), wide], axis=2)


def sibling(value):
    return swap(value, "core", 1)


def plane_perm(masks):
    parts = lax.axis_size("pd")
    return [
        (core * parts + pd, core * parts + (pd ^ masks[core]))
        for core in range(CORES)
        for pd in range(parts)
    ]


def pack(sketch, logit):
    high = logit.astype(jnp.bfloat16)
    low = (logit - high.astype(jnp.float32)).astype(jnp.bfloat16)
    return jnp.concatenate([sketch.astype(jnp.bfloat16), high, low], axis=-1)


def add_packed(sketch, logit, packed):
    width, lanes = sketch.shape[-1], logit.shape[-1]
    high, low = packed[..., width : width + lanes], packed[..., width + lanes :]
    return (
        sketch + packed[..., :width].astype(jnp.float32),
        logit + (high.astype(jnp.float32) + low.astype(jnp.float32)),
    )


def ring_order(rows):
    parts, chips = lax.axis_size("pd"), lax.axis_size("chip")
    place, core = lax.axis_index("chip"), lax.axis_index("core")
    per = rows // (CORES * chips)
    row = jnp.arange(rows)
    at_layer, at_core, at = row // (CORES * per), row // per % CORES, row % per
    return ((at_core != core) * chips + (place - at_layer) % chips) * per + at


def piped_sketches(
    states, gate_weight, up_weight, wvec, table, sketch_in, sketch_out, rows, length, extras
):
    parts, chips = lax.axis_size("pd"), lax.axis_size("chip")
    place, core, pd = lax.axis_index("chip"), lax.axis_index("core"), lax.axis_index("pd")
    mine = states.shape[0]
    kin, kout = sketch_in.shape[0], sketch_out.shape[0]
    first, second = (2, 1), (1, 2)
    plane = ("core", "pd")
    tie = lax.optimization_barrier

    def send_a(value):
        return lax.ppermute(value, plane, plane_perm(first))

    def send_b(value):
        return lax.ppermute(value, plane, plane_perm(second))

    def ring(value, shift=1):
        return turn(value, "chip", shift)

    sin = sketch_in.reshape(parts, kin // parts, -1)[jnp.arange(parts) ^ pd]
    sin = sin.reshape(sketch_in.shape)

    def run(*pieces):
        return layer(pieces, gate_weight, up_weight, sin, sketch_out, wvec, length)

    p0 = states
    p0s = sibling(p0)
    a0, b0, p1 = send_a(p0), send_b(p0), ring(p0)
    a0, b0, table, wvec, sin, extras = tie((a0, b0, table, wvec, sin, extras))
    a0s, b0s = sibling(a0), sibling(b0)
    a1, b1, p2 = send_a(p1), send_b(p1), ring(p1)
    d0 = send_b(a0)
    out0 = run(p0, p0s, a0, a0s, b0, b0s)
    p1s = sibling(p1)
    a1, b1, p2, out0 = tie((a1, b1, p2, out0))
    a2, b2, p3 = send_a(p2), send_b(p2), ring(p2)
    d1, d3 = send_b(a1), ring(d0, -1)
    a1s, b1s, d0s = sibling(a1), sibling(b1), sibling(d0)
    out1 = run(d0, d0s, p1, p1s, a1, a1s, b1, b1s)
    p2s = sibling(p2)
    a2, b2, p3, out1 = tie((a2, b2, p3, out1))
    a3, b3, d2 = send_a(p3), send_b(p3), ring(d1)
    a2s, b2s, d1s = sibling(a2), sibling(b2), sibling(d1)
    out2 = run(d1, d1s, p2, p2s, a2, a2s, b2, b2s)
    p3s = sibling(p3)
    a3, b3, d2, d3, out2 = tie((a3, b3, d2, d3, out2))
    out3 = run(
        d2, sibling(d2), p3, p3s, a3, sibling(a3), b3, sibling(b3), d3, sibling(d3)
    )
    outs = (out0, out1, out2, out3)

    cores = (core + jnp.arange(CORES)) % CORES
    apart = jnp.arange(parts)[None, :] ^ pd
    is_a = jnp.where(cores[:, None] == 0, apart == first[0], apart == first[1])
    slot = jnp.where(apart == 0, 0, jnp.where(apart == 3, 6, jnp.where(is_a, 2, 4)))
    slot = slot + jnp.arange(CORES)[:, None]
    order = slot[:, None, :] + 2 * parts * jnp.arange(chips)[None, :, None]
    order = order.reshape(-1)
    pieces = order.shape[0]
    proj = jnp.concatenate([o[0] for o in outs]).reshape(pieces, -1, kin + kout)[order]
    logit = jnp.concatenate([o[1] for o in outs]).reshape(pieces, -1, 8 * 128).sum(axis=2)[order]
    proj = proj.reshape(rows, length, kin + kout)
    sketch = jnp.einsum(
        "rti,rto->rio", proj[:, :, :kin], proj[:, :, kin:], precision=lax.Precision.HIGHEST
    )
    part = add_logit(sketch.reshape(rows, kin * kout), logit.reshape(rows), parts)
    half = part[: rows // CORES] + sibling(part[rows // CORES :])
    width = half.shape[2] - 128
    sketch, logit = half[:, 0, :width], half[:, 0, width : width + 64]
    for k in range(1, parts):
        packed = pack(half[:, k, :width], half[:, k, width : width + 64])
        sketch, logit = add_packed(sketch, logit, swap(packed, "pd", k))
    sketch, logit = (v.reshape(chips, -1, v.shape[1]) for v in (sketch, logit))
    packed = pack(sketch, logit)
    for k in range(1, chips):
        sketch, logit = add_packed(sketch, logit, jnp.roll(ring(packed, k), k, axis=0))
    whole = jnp.concatenate([sketch, logit, logit], axis=-1).reshape(rows // CORES, -1)
    both = jnp.concatenate([whole, sibling(whole)])
    return both, table, extras


def contrast_kernel(with_table, diff, *refs):
    step = pl.program_id(0)
    lead = 1 if with_table else 0
    table, store, outs = (refs[0], refs[1], refs[2:]) if with_table else (None, refs[0], refs[1:])
    mine = outs[0].shape[0]

    if with_table:

        @pl.when(step == 0)
        def _():
            both = lax.dot_general(
                table[...], diff[...], CONTRACT, preferred_element_type=jnp.float32
            ).T
            half = both.shape[1] // 2
            score = both[:, :half] + both[:, half:]
            high = score.astype(jnp.bfloat16)
            low = (score - high.astype(jnp.float32)).astype(jnp.bfloat16)
            for i, out in enumerate(outs):
                out[:, :half] = high[i * mine : (i + 1) * mine]
                out[:, half:] = low[i * mine : (i + 1) * mine]

    @pl.when(step >= lead)
    def _():
        part = lax.dot_general(
            store[...], diff[...], CONTRACT, preferred_element_type=jnp.float32
        ).T
        for i, out in enumerate(outs):
            out[...] = part[i * mine : (i + 1) * mine].astype(out.dtype)


def contrast_parts(diff, store, first, blocks, parts, table=None):
    rows, width = diff.shape
    block = 2 * SOURCES
    lead = 0 if table is None else 1
    mine = rows // parts
    columns = block * (blocks + lead)
    tables = [] if table is None else [table]
    return pl.pallas_call(
        functools.partial(contrast_kernel, table is not None),
        grid=(blocks + lead,),
        in_specs=[pl.BlockSpec((rows, width), lambda k: (0, 0))]
        + [pl.BlockSpec((block, width), lambda k: (0, 0))] * lead
        + [pl.BlockSpec((block, width), lambda k: (first + jnp.maximum(k - lead, 0), 0))],
        out_specs=[pl.BlockSpec((mine, block), lambda k: (0, k))] * parts,
        out_shape=[jax.ShapeDtypeStruct((mine, columns), jnp.bfloat16)] * parts,
        compiler_params=pltpu.CompilerParams(vmem_limit_bytes=60 * 1024 * 1024),
        cost_estimate=pl.CostEstimate(
            flops=2 * rows * width * columns,
            bytes_accessed=2 * (width + rows) * columns,
            transcendentals=0,
        ),
    )(diff, *tables, store)


def exchange(blocks):
    total = blocks[0].astype(jnp.float32)
    for k in range(1, len(blocks)):
        total = total + swap(blocks[k], "pd", k).astype(jnp.float32)
    return total


def plain_sketches(
    states, gate_weight, up_weight, wvec, table, sketch_in, sketch_out, rows, length, extras
):
    kin, kout = sketch_in.shape[0], sketch_out.shape[0]
    ff_local = gate_weight.shape[1]
    states = lax.all_gather(states, ("chip", "core", "pd"), axis=0, tiled=True)
    gate = jnp.dot(states, gate_weight, preferred_element_type=jnp.float32)
    up = jnp.dot(states, up_weight, preferred_element_type=jnp.float32)
    ain = lax.dot_general(states, sketch_in, CONTRACT, preferred_element_type=jnp.float32)
    sig = jax.nn.sigmoid(gate)
    weighted = up * wvec
    logit = jnp.sum((gate * sig * weighted).reshape(rows, length * ff_local), axis=1)
    dgate = (weighted * sig * (1.0 + gate * (1.0 - sig))).astype(jnp.bfloat16)
    bout = lax.dot_general(dgate, sketch_out, CONTRACT, preferred_element_type=jnp.float32)
    sketch = jnp.einsum(
        "rti,rto->rio",
        ain.reshape(rows, length, kin),
        bout.reshape(rows, length, kout),
        precision=lax.Precision.HIGHEST,
    ).reshape(rows, kin * kout)
    reduced = reduce_rows(add_logit(sketch, logit, lax.axis_size("pd")))
    return reduced, table, extras


def on_device(
    verdict_states,
    verdict_labels,
    partner,
    gate_weight,
    up_weight,
    down_weight,
    readout,
    sketch_in,
    sketch_out,
    store,
    source_ids,
):
    rows = verdict_labels.shape[0]
    parts, chips = lax.axis_size("pd"), lax.axis_size("chip")
    pd = lax.axis_index("pd")
    examples, width = store.shape
    mine = verdict_states.shape[0]
    length = mine * parts * CORES * chips // rows

    wvec = jnp.dot(down_weight, readout, preferred_element_type=jnp.float32)[None, :]
    table = source_table(store, source_ids)
    piped = (
        parts == 4
        and chips == 4
        and mine == 2 * length
        and length == 32
        and gate_weight.shape[1] % 128 == 0
        and gate_weight.shape[0] % 1024 == 0
    )
    sketches = piped_sketches if piped else plain_sketches
    index = ring_order(rows) if piped else jnp.arange(rows)
    group = rows // parts
    order = jnp.concatenate([(pd ^ k) * group + jnp.arange(group) for k in range(parts)])
    labels = jnp.zeros_like(verdict_labels).at[index].set(verdict_labels)
    sign = 2.0 * labels.astype(jnp.float32) - 1.0
    extras = (sign, index[order], index[partner[order]])
    reduced, table, extras = sketches(
        verdict_states,
        gate_weight,
        up_weight,
        wvec,
        table,
        sketch_in,
        sketch_out,
        rows,
        length,
        extras,
    )
    sign, mine_at, mate_at = extras

    coef = -sign * jax.nn.sigmoid(-sign * (reduced[:, width] / length))
    scaled = reduced[:, :width] * (coef / length)[:, None]
    diff = (scaled[mine_at] - scaled[mate_at]).astype(jnp.bfloat16)

    blocks = examples // (2 * SOURCES)
    early = blocks // 2
    front = exchange(contrast_parts(diff, store, 0, early, parts, table))
    back = exchange(contrast_parts(diff, store, early, blocks - early, parts))
    scores = front[:, :SOURCES] + front[:, SOURCES : 2 * SOURCES]
    whole = scores
    for k in range(1, chips):
        whole = whole + turn(scores, "chip", k)
    whole = whole + sibling(whole)
    factor = (SOURCES / (examples * CORES * chips)) ** 0.5
    contrast = jnp.concatenate([front[:, 2 * SOURCES :], back], axis=1)
    return (contrast, whole * factor)


def solution(mesh):
    ex, pd = mesh.shape["ex"], mesh.shape["pd"]
    axed = Mesh(mesh.devices.reshape(ex // CORES, CORES, pd), ("chip", "core", "pd"))
    every = ("chip", "core", "pd")
    in_specs = (
        P(every, None),
        P(),
        P(),
        P(None, every),
        P(None, every),
        P(every, None),
        P(),
        P(),
        P(None, every),
        P(("chip", "core"), "pd"),
        P(("chip", "core")),
    )
    out_specs = (P("pd", ("chip", "core")), P("pd", None))
    return jax.shard_map(
        on_device, mesh=axed, in_specs=in_specs, out_specs=out_specs, check_vma=False
    )
```

```python
import functools

import jax
import jax.numpy as jnp
from jax import lax
from jax.experimental import pallas as pl
from jax.experimental.pallas import tpu as pltpu
from jax.sharding import Mesh
from jax.sharding import PartitionSpec as P

SOURCES = 512
CORES = 2
SPLIT = 4
CONTRACT = (((1,), (1,)), ((), ()))


def swap(value, axis, mask):
    size = lax.axis_size(axis)
    return lax.ppermute(value, axis, [(i, i ^ mask) for i in range(size)])


def turn(value, axis, shift):
    size = lax.axis_size(axis)
    return lax.ppermute(value, axis, [(i, (i + shift) % size) for i in range(size)])


def pick(value, index, axis):
    return lax.dynamic_index_in_dim(value, index, axis, keepdims=False)


def reduce_rows(part):
    rows, parts, width = part.shape
    core, pd = lax.axis_index("core"), lax.axis_index("pd")
    halves = part.reshape(CORES, rows // CORES, parts, width)
    half = pick(halves, core, 0) + swap(pick(halves, 1 - core, 0), "core", 1)
    total = pick(half, pd, 1)
    for k in range(1, parts):
        total = total + swap(pick(half, pd ^ k, 1), "pd", k)
    whole = total
    for k in range(1, lax.axis_size("chip")):
        whole = whole + turn(total, "chip", k)
    other = swap(whole, "core", 1)
    first = jnp.where(core == 0, whole, other)
    second = jnp.where(core == 0, other, whole)
    return jnp.concatenate([first, second], axis=0)


def layer_kernel(count, length, cuts, *refs):
    pieces = refs[:count]
    gate_w, up_w, sin, sout, wvec, proj, lrow, x, w, acc, dgate, sems, x_sems = refs[count:]
    step = pl.program_id(0)
    steps = pl.num_programs(0)
    block = w.shape[1]
    features = gate_w.shape[1]
    tokens = pieces[0].shape[0]
    kin = sin.shape[0]

    def copies(k):
        slot = lax.rem(k, 2)
        part = block // SPLIT
        return [
            pltpu.make_async_copy(
                weight.at[pl.ds(pl.multiple_of(k * block + h * part, part), part), :],
                w.at[slot, pl.ds(h * part, part), pl.ds(i * features, features)],
                sems.at[slot, i, h],
            )
            for h in range(SPLIT)
            for i, weight in enumerate((gate_w, up_w))
        ]

    def piece_copies(part):
        at = pl.ds(cuts[part] * block, (cuts[part + 1] - cuts[part]) * block)
        return [
            pltpu.make_async_copy(
                piece.at[:, at], x.at[pl.ds(i * tokens, tokens), at], x_sems.at[part, i]
            )
            for i, piece in enumerate(pieces)
        ]

    @pl.when(step == 0)
    def _():
        for copy in copies(step):
            copy.start()
        for copy in piece_copies(0):
            copy.start()

    @pl.when(step + 1 < steps)
    def _():
        for copy in copies(step + 1):
            copy.start()

    @pl.when(step == 0)
    def _():
        for part in range(1, len(cuts) - 1):
            for copy in piece_copies(part):
                copy.start()
        acc[...] = jnp.zeros_like(acc)
        proj[...] = jnp.zeros_like(proj)

    for copy in copies(step):
        copy.wait()
    for part in range(len(cuts) - 1):

        @pl.when(step == cuts[part])
        def _():
            for copy in piece_copies(part):
                copy.wait()

    now = x[:, pl.ds(pl.multiple_of(step * block, block), block)]
    proj[:, :kin] += lax.dot_general(now, sin[...], CONTRACT, preferred_element_type=jnp.float32)
    acc[...] += jnp.dot(now, w[lax.rem(step, 2)], preferred_element_type=jnp.float32)

    @pl.when(step == steps - 1)
    def _():
        @pl.loop(0, acc.shape[0] // length)
        def _(i):
            here = pl.ds(pl.multiple_of(i * length, length), length)
            total = jnp.zeros((length, 128), jnp.float32)
            for j in range(features // 128):
                at = slice(j * 128, (j + 1) * 128)
                gate = acc[here, at]
                weighted = acc[here, features + j * 128 : features + (j + 1) * 128] * wvec[:, at]
                sig = jax.nn.sigmoid(gate)
                swish = gate * sig
                total = total + swish * weighted
                dgate[here, at] = (weighted * (sig + swish * (1.0 - sig))).astype(jnp.bfloat16)
            lrow[pl.ds(pl.multiple_of(8 * i, 8), 8), :] = total.reshape(-1, 8, 128).sum(axis=0)

        proj[:, kin:] = lax.dot_general(
            dgate[...], sout[...], CONTRACT, preferred_element_type=jnp.float32
        )


def layer(pieces, gate_weight, up_weight, sketch_in, sketch_out, wvec, length):
    count = len(pieces)
    tokens, depth = pieces[0].shape
    total = count * tokens
    features = gate_weight.shape[1]
    kin, kout = sketch_in.shape[0], sketch_out.shape[0]
    rows = total // length
    block = min(1024, depth)
    steps = depth // block
    cuts = (0, 1, 3, steps)
    return pl.pallas_call(
        functools.partial(layer_kernel, count, length, cuts),
        grid=(steps,),
        in_specs=[pl.BlockSpec(memory_space=pl.ANY)] * (count + 2)
        + [
            pl.BlockSpec((kin, block), lambda k: (0, k)),
            pl.BlockSpec((kout, features), lambda k: (0, 0)),
            pl.BlockSpec((1, features), lambda k: (0, 0)),
        ],
        out_specs=[
            pl.BlockSpec((total, kin + kout), lambda k: (0, 0)),
            pl.BlockSpec((rows * 8, 128), lambda k: (0, 0)),
        ],
        out_shape=[
            jax.ShapeDtypeStruct((total, kin + kout), jnp.float32),
            jax.ShapeDtypeStruct((rows * 8, 128), jnp.float32),
        ],
        scratch_shapes=[
            pltpu.VMEM((total, depth), jnp.bfloat16),
            pltpu.VMEM((2, block, 2 * features), jnp.bfloat16),
            pltpu.VMEM((total, 2 * features), jnp.float32),
            pltpu.VMEM((total, features), jnp.bfloat16),
            pltpu.SemaphoreType.DMA((2, 2, SPLIT)),
            pltpu.SemaphoreType.DMA((len(cuts) - 1, count)),
        ],
        compiler_params=pltpu.CompilerParams(vmem_limit_bytes=60 * 1024 * 1024),
        cost_estimate=pl.CostEstimate(
            flops=4 * total * depth * features,
            bytes_accessed=2 * depth * (2 * features + total),
            transcendentals=total * features,
        ),
    )(*pieces, gate_weight, up_weight, sketch_in, sketch_out, wvec)


def prepare_kernel(ids, readout, *refs):
    stores, downs = refs[:SPLIT], refs[SPLIT : 2 * SPLIT]
    table, wvec, acc = refs[2 * SPLIT :]
    step = pl.program_id(0)

    @pl.when(step == 0)
    def _():
        acc[...] = jnp.zeros_like(acc)
        wvec[...] = jnp.zeros_like(wvec)

    sources = acc.shape[0]
    part = stores[0].shape[0]
    labels = lax.broadcasted_iota(jnp.int32, (sources, part), 0)
    for i, store in enumerate(stores):
        onehot = jnp.where(labels == ids[:, i * part : (i + 1) * part], 1.0, 0.0)
        acc[...] += jnp.dot(
            onehot.astype(jnp.bfloat16), store[...], preferred_element_type=jnp.float32
        )
    for i, down in enumerate(downs):
        wvec[i] += lax.dot_general(
            readout[...], down[...], CONTRACT, preferred_element_type=jnp.float32
        )

    @pl.when(step == pl.num_programs(0) - 1)
    def _():
        high = acc[...].astype(jnp.bfloat16)
        table[:sources, :] = high
        table[sources:, :] = (acc[...] - high.astype(jnp.float32)).astype(jnp.bfloat16)


def prepare(store, source_ids, down_weight, readout):
    examples, width = store.shape
    features, depth = down_weight.shape
    steps = 8
    block, deep = examples // steps, depth // steps
    part, piece = block // SPLIT, features // SPLIT
    table, wvec = pl.pallas_call(
        prepare_kernel,
        grid=(steps,),
        in_specs=[
            pl.BlockSpec((1, block), lambda k: (0, k)),
            pl.BlockSpec((8, deep), lambda k: (0, k)),
        ]
        + [pl.BlockSpec((part, width), lambda k, i=i: (k * SPLIT + i, 0)) for i in range(SPLIT)]
        + [pl.BlockSpec((piece, deep), lambda k, i=i: (i, k)) for i in range(SPLIT)],
        out_specs=[
            pl.BlockSpec((2 * SOURCES, width), lambda k: (0, 0)),
            pl.BlockSpec((SPLIT, 8, piece), lambda k: (0, 0, 0)),
        ],
        out_shape=[
            jax.ShapeDtypeStruct((2 * SOURCES, width), jnp.bfloat16),
            jax.ShapeDtypeStruct((SPLIT, 8, piece), jnp.float32),
        ],
        scratch_shapes=[pltpu.VMEM((SOURCES, width), jnp.float32)],
        compiler_params=pltpu.CompilerParams(vmem_limit_bytes=60 * 1024 * 1024),
        cost_estimate=pl.CostEstimate(
            flops=2 * SOURCES * examples * width,
            bytes_accessed=2 * examples * width + 2 * features * depth,
            transcendentals=0,
        ),
    )(
        source_ids.reshape(1, -1),
        jnp.broadcast_to(readout[None, :], (8, depth)),
        *[store] * SPLIT,
        *[down_weight] * SPLIT,
    )
    return table, wvec[:, 0].reshape(1, features)


def add_logit(sketch, logit, parts):
    rows = sketch.shape[0]
    wide = jnp.broadcast_to(logit[:, None, None], (rows, parts, 128))
    return jnp.concatenate([sketch.reshape(rows, parts, -1), wide], axis=2)


def sibling(value):
    return swap(value, "core", 1)


def plane_perm(masks):
    parts = lax.axis_size("pd")
    return [
        (core * parts + pd, core * parts + (pd ^ masks[core]))
        for core in range(CORES)
        for pd in range(parts)
    ]


def pack(sketch, logit):
    high = logit.astype(jnp.bfloat16)
    low = (logit - high.astype(jnp.float32)).astype(jnp.bfloat16)
    return jnp.concatenate([sketch.astype(jnp.bfloat16), high, low], axis=-1)


def add_packed(sketch, logit, packed):
    width, lanes = sketch.shape[-1], logit.shape[-1]
    high, low = packed[..., width : width + lanes], packed[..., width + lanes :]
    return (
        sketch + packed[..., :width].astype(jnp.float32),
        logit + (high.astype(jnp.float32) + low.astype(jnp.float32)),
    )


def ring_order(rows):
    parts, chips = lax.axis_size("pd"), lax.axis_size("chip")
    place, core = lax.axis_index("chip"), lax.axis_index("core")
    per = rows // (CORES * chips)
    row = jnp.arange(rows)
    at_layer, at_core, at = row // (CORES * per), row // per % CORES, row % per
    return ((at_core != core) * chips + (place - at_layer) % chips) * per + at


def piped_sketches(
    states, gate_weight, up_weight, wvec, table, sketch_in, sketch_out, rows, length, extras
):
    parts, chips = lax.axis_size("pd"), lax.axis_size("chip")
    place, core, pd = lax.axis_index("chip"), lax.axis_index("core"), lax.axis_index("pd")
    mine = states.shape[0]
    kin, kout = sketch_in.shape[0], sketch_out.shape[0]
    first, second = (2, 1), (1, 2)
    plane = ("core", "pd")
    tie = lax.optimization_barrier

    def send_a(value):
        return lax.ppermute(value, plane, plane_perm(first))

    def send_b(value):
        return lax.ppermute(value, plane, plane_perm(second))

    def ring(value, shift=1):
        return turn(value, "chip", shift)

    sin = sketch_in.reshape(parts, kin // parts, -1)[jnp.arange(parts) ^ pd]
    sin = sin.reshape(sketch_in.shape)

    def run(*pieces):
        return layer(pieces, gate_weight, up_weight, sin, sketch_out, wvec, length)

    p0 = states
    p0s = sibling(p0)
    a0, b0, p1 = send_a(p0), send_b(p0), ring(p0)
    a0, b0, table, wvec, sin, extras = tie((a0, b0, table, wvec, sin, extras))
    a0s, b0s = sibling(a0), sibling(b0)
    a1, b1, p2 = send_a(p1), send_b(p1), ring(p1)
    d0 = send_b(a0)
    a0s, p0 = tie((a0s, p0))
    p3 = ring(p0, -1)
    out0 = run(p0, p0s, a0, a0s, b0, b0s)
    p1s = sibling(p1)
    p2, p3, out0 = tie((p2, p3, out0))
    a2, b2, p2s = send_a(p2), send_b(p2), sibling(p2)
    a1, b1, p2s = tie((a1, b1, p2s))
    d1, d3 = send_b(a1), ring(d0, -1)
    a1s, b1s, d0s = sibling(a1), sibling(b1), sibling(d0)
    out1 = run(d0, d0s, p1, p1s, a1, a1s, b1, b1s)
    a2, b2, d1, out1 = tie((a2, b2, d1, out1))
    p3 = tie((p3, out1))[0]
    a3, b3, d2 = send_a(p3), send_b(p3), ring(d1)
    a2s, b2s, d1s = sibling(a2), sibling(b2), sibling(d1)
    d1s, d3 = tie((d1s, d3))
    out2 = run(d1, d1s, p2, p2s, a2, a2s, b2, b2s)
    p3s = sibling(p3)
    a3, b3, d2, out2 = tie((a3, b3, d2, out2))
    out3 = run(
        d2, sibling(d2), p3, p3s, a3, sibling(a3), b3, sibling(b3), d3, sibling(d3)
    )
    outs = (out0, out1, out2, out3)

    cores = (core + jnp.arange(CORES)) % CORES
    apart = jnp.arange(parts)[None, :] ^ pd
    is_a = jnp.where(cores[:, None] == 0, apart == first[0], apart == first[1])
    slot = jnp.where(apart == 0, 0, jnp.where(apart == 3, 6, jnp.where(is_a, 2, 4)))
    slot = slot + jnp.arange(CORES)[:, None]
    order = slot[:, None, :] + 2 * parts * jnp.arange(chips)[None, :, None]
    order = order.reshape(-1)
    pieces = order.shape[0]
    proj = jnp.concatenate([o[0] for o in outs]).reshape(pieces, -1, kin + kout)[order]
    logit = jnp.concatenate([o[1] for o in outs]).reshape(pieces, -1, 8 * 128).sum(axis=2)[order]
    proj = proj.reshape(rows, length, kin + kout)
    sketch = jnp.einsum(
        "rti,rto->rio", proj[:, :, :kin], proj[:, :, kin:], precision=lax.Precision.HIGHEST
    )
    part = add_logit(sketch.reshape(rows, kin * kout), logit.reshape(rows), parts)
    half = part[: rows // CORES] + sibling(part[rows // CORES :])
    width = half.shape[2] - 128
    sketch, logit = half[:, 0, :width], half[:, 0, width : width + 64]
    for k in range(1, parts):
        packed = pack(half[:, k, :width], half[:, k, width : width + 64])
        sketch, logit = add_packed(sketch, logit, swap(packed, "pd", k))
    sketch, logit = (v.reshape(chips, -1, v.shape[1]) for v in (sketch, logit))
    packed = pack(sketch, logit)
    for k in range(1, chips):
        sketch, logit = add_packed(sketch, logit, jnp.roll(ring(packed, k), k, axis=0))
    whole = jnp.concatenate([sketch, logit, logit], axis=-1).reshape(rows // CORES, -1)
    both = jnp.concatenate([whole, sibling(whole)])
    return both, table, extras


def contrast_kernel(with_table, diff, *refs):
    step = pl.program_id(0)
    lead = 1 if with_table else 0
    table, stores, outs = refs[:lead], refs[lead : lead + SPLIT], refs[lead + SPLIT :]
    mine = outs[0].shape[0]

    if with_table:

        @pl.when(step == 0)
        def _():
            both = lax.dot_general(
                table[0][...], diff[...], CONTRACT, preferred_element_type=jnp.float32
            ).T
            half = both.shape[1] // 2
            score = both[:, :half] + both[:, half:]
            high = score.astype(jnp.bfloat16)
            low = (score - high.astype(jnp.float32)).astype(jnp.bfloat16)
            for i, out in enumerate(outs):
                out[:, :half] = high[i * mine : (i + 1) * mine]
                out[:, half:] = low[i * mine : (i + 1) * mine]

    @pl.when(step >= lead)
    def _():
        for j, store in enumerate(stores):
            part = lax.dot_general(
                store[...], diff[...], CONTRACT, preferred_element_type=jnp.float32
            ).T
            size = part.shape[1]
            for i, out in enumerate(outs):
                out[:, j * size : (j + 1) * size] = part[i * mine : (i + 1) * mine].astype(
                    out.dtype
                )


def contrast_parts(diff, store, first, blocks, parts, table=None):
    rows, width = diff.shape
    block = 2 * SOURCES
    lead = 0 if table is None else 1
    mine = rows // parts
    columns = block * (blocks + lead)
    tables = [] if table is None else [table]

    def stored(i):
        return pl.BlockSpec(
            (block // SPLIT, width),
            lambda k: ((first + jnp.maximum(k - lead, 0)) * SPLIT + i, 0),
        )

    return pl.pallas_call(
        functools.partial(contrast_kernel, table is not None),
        grid=(blocks + lead,),
        in_specs=[pl.BlockSpec((rows, width), lambda k: (0, 0))]
        + [pl.BlockSpec((block, width), lambda k: (0, 0))] * lead
        + [stored(i) for i in range(SPLIT)],
        out_specs=[pl.BlockSpec((mine, block), lambda k: (0, k))] * parts,
        out_shape=[jax.ShapeDtypeStruct((mine, columns), jnp.bfloat16)] * parts,
        compiler_params=pltpu.CompilerParams(vmem_limit_bytes=60 * 1024 * 1024),
        cost_estimate=pl.CostEstimate(
            flops=2 * rows * width * columns,
            bytes_accessed=2 * (width + rows) * columns,
            transcendentals=0,
        ),
    )(diff, *tables, *[store] * SPLIT)


def exchange(blocks):
    total = blocks[0].astype(jnp.float32)
    for k in range(1, len(blocks)):
        total = total + swap(blocks[k], "pd", k).astype(jnp.float32)
    return total


def plain_sketches(
    states, gate_weight, up_weight, wvec, table, sketch_in, sketch_out, rows, length, extras
):
    kin, kout = sketch_in.shape[0], sketch_out.shape[0]
    ff_local = gate_weight.shape[1]
    states = lax.all_gather(states, ("chip", "core", "pd"), axis=0, tiled=True)
    gate = jnp.dot(states, gate_weight, preferred_element_type=jnp.float32)
    up = jnp.dot(states, up_weight, preferred_element_type=jnp.float32)
    ain = lax.dot_general(states, sketch_in, CONTRACT, preferred_element_type=jnp.float32)
    sig = jax.nn.sigmoid(gate)
    weighted = up * wvec
    logit = jnp.sum((gate * sig * weighted).reshape(rows, length * ff_local), axis=1)
    dgate = (weighted * sig * (1.0 + gate * (1.0 - sig))).astype(jnp.bfloat16)
    bout = lax.dot_general(dgate, sketch_out, CONTRACT, preferred_element_type=jnp.float32)
    sketch = jnp.einsum(
        "rti,rto->rio",
        ain.reshape(rows, length, kin),
        bout.reshape(rows, length, kout),
        precision=lax.Precision.HIGHEST,
    ).reshape(rows, kin * kout)
    reduced = reduce_rows(add_logit(sketch, logit, lax.axis_size("pd")))
    return reduced, table, extras


def on_device(
    verdict_states,
    verdict_labels,
    partner,
    gate_weight,
    up_weight,
    down_weight,
    readout,
    sketch_in,
    sketch_out,
    store,
    source_ids,
):
    rows = verdict_labels.shape[0]
    parts, chips = lax.axis_size("pd"), lax.axis_size("chip")
    pd = lax.axis_index("pd")
    examples, width = store.shape
    mine = verdict_states.shape[0]
    length = mine * parts * CORES * chips // rows

    table, wvec = prepare(store, source_ids, down_weight, readout)
    piped = (
        parts == 4
        and chips == 4
        and mine == 2 * length
        and length == 32
        and gate_weight.shape[1] % 128 == 0
        and gate_weight.shape[0] % 1024 == 0
        and gate_weight.shape[0] > 3072
    )
    sketches = piped_sketches if piped else plain_sketches
    index = ring_order(rows) if piped else jnp.arange(rows)
    group = rows // parts
    order = jnp.concatenate([(pd ^ k) * group + jnp.arange(group) for k in range(parts)])
    labels = jnp.zeros_like(verdict_labels).at[index].set(verdict_labels)
    sign = 2.0 * labels.astype(jnp.float32) - 1.0
    extras = (sign, index[order], index[partner[order]])
    reduced, table, extras = sketches(
        verdict_states,
        gate_weight,
        up_weight,
        wvec,
        table,
        sketch_in,
        sketch_out,
        rows,
        length,
        extras,
    )
    sign, mine_at, mate_at = extras

    coef = -sign * jax.nn.sigmoid(-sign * (reduced[:, width] / length))
    scaled = reduced[:, :width] * (coef / length)[:, None]
    diff = (scaled[mine_at] - scaled[mate_at]).astype(jnp.bfloat16)

    blocks = examples // (2 * SOURCES)
    early = blocks // 2
    front = exchange(contrast_parts(diff, store, 0, early, parts, table))
    back = exchange(contrast_parts(diff, store, early, blocks - early, parts))
    scores = front[:, :SOURCES] + front[:, SOURCES : 2 * SOURCES]
    whole = scores
    for k in range(1, chips):
        whole = whole + turn(scores, "chip", k)
    whole = whole + sibling(whole)
    factor = (SOURCES / (examples * CORES * chips)) ** 0.5
    contrast = jnp.concatenate([front[:, 2 * SOURCES :], back], axis=1)
    return (contrast, whole * factor)


def solution(mesh):
    ex, pd = mesh.shape["ex"], mesh.shape["pd"]
    axed = Mesh(mesh.devices.reshape(ex // CORES, CORES, pd), ("chip", "core", "pd"))
    every = ("chip", "core", "pd")
    in_specs = (
        P(every, None),
        P(),
        P(),
        P(None, every),
        P(None, every),
        P(every, None),
        P(),
        P(),
        P(None, every),
        P(("chip", "core"), "pd"),
        P(("chip", "core")),
    )
    out_specs = (P("pd", ("chip", "core")), P("pd", None))
    return jax.shard_map(
        on_device, mesh=axed, in_specs=in_specs, out_specs=out_specs, check_vma=False
    )
```

```python
import functools

import jax
import jax.numpy as jnp
from jax import lax
from jax.experimental import pallas as pl
from jax.experimental.pallas import tpu as pltpu
from jax.sharding import Mesh
from jax.sharding import PartitionSpec as P

SOURCES = 512
CORES = 2
SPLIT = 4
CONTRACT = (((1,), (1,)), ((), ()))


def swap(value, axis, mask):
    size = lax.axis_size(axis)
    return lax.ppermute(value, axis, [(i, i ^ mask) for i in range(size)])


def turn(value, axis, shift):
    size = lax.axis_size(axis)
    return lax.ppermute(value, axis, [(i, (i + shift) % size) for i in range(size)])


def pick(value, index, axis):
    return lax.dynamic_index_in_dim(value, index, axis, keepdims=False)


def reduce_rows(part):
    rows, parts, width = part.shape
    core, pd = lax.axis_index("core"), lax.axis_index("pd")
    halves = part.reshape(CORES, rows // CORES, parts, width)
    half = pick(halves, core, 0) + swap(pick(halves, 1 - core, 0), "core", 1)
    total = pick(half, pd, 1)
    for k in range(1, parts):
        total = total + swap(pick(half, pd ^ k, 1), "pd", k)
    whole = total
    for k in range(1, lax.axis_size("chip")):
        whole = whole + turn(total, "chip", k)
    other = swap(whole, "core", 1)
    first = jnp.where(core == 0, whole, other)
    second = jnp.where(core == 0, other, whole)
    return jnp.concatenate([first, second], axis=0)


def layer_kernel(count, length, block, *refs):
    pieces = refs[:count]
    gate_w, up_w, sin_hbm, sout, wvec, proj, lrow, x, w, sin, acc, dgate, sems, x_sems = refs[count:]
    depth, features = gate_w.shape
    tokens = pieces[0].shape[0]
    kin = sin.shape[0]
    steps = depth // block
    cuts = (0, 1, 3, steps)

    def copies(k):
        here = pl.ds(pl.multiple_of(k * block, block), block)
        return [
            pltpu.make_async_copy(
                weight.at[here, :], w.at[here, pl.ds(i * features, features)], sems.at[k, i]
            )
            for i, weight in enumerate((gate_w, up_w))
        ]

    def piece_copies(part):
        at = pl.ds(cuts[part] * block, (cuts[part + 1] - cuts[part]) * block)
        return [
            pltpu.make_async_copy(
                piece.at[:, at], x.at[pl.ds(i * tokens, tokens), at], x_sems.at[part, i]
            )
            for i, piece in enumerate(pieces)
        ]

    sin_copy = pltpu.make_async_copy(sin_hbm, sin, sems.at[steps, 0])
    for k in range(steps):
        for copy in copies(k):
            copy.start()
        for part in range(len(cuts) - 1):
            if cuts[part] == k:
                for copy in piece_copies(part):
                    copy.start()
    sin_copy.start()

    def product(k, span):
        at = pl.ds(pl.multiple_of(k * block, block), span * block)
        return jnp.dot(x[:, at], w[at, :], preferred_element_type=jnp.float32)

    for copy in copies(0) + piece_copies(0):
        copy.wait()
    acc[...] = product(0, 1)

    @pl.loop(0, (steps - 2) // 2)
    def _(i):
        k = 2 * i + 1
        for copy in copies(k) + copies(k + 1):
            copy.wait()

        @pl.when(i == 0)
        def _():
            for copy in piece_copies(1):
                copy.wait()

        @pl.when(i == 1)
        def _():
            for copy in piece_copies(2):
                copy.wait()

        acc[...] += product(k, 2)

    for copy in copies(steps - 1):
        copy.wait()
    sin_copy.wait()
    acc[...] += product(steps - 1, 1)
    proj[:, :kin] = lax.dot_general(x[...], sin[...], CONTRACT, preferred_element_type=jnp.float32)

    @pl.loop(0, acc.shape[0] // length)
    def _(i):
        here = pl.ds(pl.multiple_of(i * length, length), length)
        total = jnp.zeros((length, 128), jnp.float32)
        for j in range(features // 128):
            at = slice(j * 128, (j + 1) * 128)
            gate = acc[here, at]
            weighted = acc[here, features + j * 128 : features + (j + 1) * 128] * wvec[:, at]
            sig = jax.nn.sigmoid(gate)
            swish = gate * sig
            total = total + swish * weighted
            dgate[here, at] = (weighted * (sig + swish * (1.0 - sig))).astype(jnp.bfloat16)
        lrow[pl.ds(pl.multiple_of(8 * i, 8), 8), :] = total.reshape(-1, 8, 128).sum(axis=0)

    proj[:, kin:] = lax.dot_general(
        dgate[...], sout[...], CONTRACT, preferred_element_type=jnp.float32
    )


def layer(pieces, gate_weight, up_weight, sketch_in, sketch_out, wvec, length):
    count = len(pieces)
    tokens, depth = pieces[0].shape
    total = count * tokens
    features = gate_weight.shape[1]
    kin, kout = sketch_in.shape[0], sketch_out.shape[0]
    rows = total // length
    block = min(1024, depth)
    steps = depth // block
    return pl.pallas_call(
        functools.partial(layer_kernel, count, length, block),
        in_specs=[pl.BlockSpec(memory_space=pl.ANY)] * (count + 3)
        + [pl.BlockSpec(memory_space=pltpu.VMEM)] * 2,
        out_specs=[pl.BlockSpec(memory_space=pltpu.VMEM)] * 2,
        out_shape=[
            jax.ShapeDtypeStruct((total, kin + kout), jnp.float32),
            jax.ShapeDtypeStruct((rows * 8, 128), jnp.float32),
        ],
        scratch_shapes=[
            pltpu.VMEM((total, depth), jnp.bfloat16),
            pltpu.VMEM((depth, 2 * features), jnp.bfloat16),
            pltpu.VMEM((kin, depth), jnp.bfloat16),
            pltpu.VMEM((total, 2 * features), jnp.float32),
            pltpu.VMEM((total, features), jnp.bfloat16),
            pltpu.SemaphoreType.DMA((steps + 1, 2)),
            pltpu.SemaphoreType.DMA((3, count)),
        ],
        compiler_params=pltpu.CompilerParams(vmem_limit_bytes=62 * 1024 * 1024),
        cost_estimate=pl.CostEstimate(
            flops=4 * total * depth * features,
            bytes_accessed=2 * depth * (2 * features + total),
            transcendentals=total * features,
        ),
    )(*pieces, gate_weight, up_weight, sketch_in, sketch_out, wvec)


def prepare_kernel(ids, readout, *refs):
    stores, downs = refs[:SPLIT], refs[SPLIT : 2 * SPLIT]
    table, wvec, acc = refs[2 * SPLIT :]
    step = pl.program_id(0)

    @pl.when(step == 0)
    def _():
        acc[...] = jnp.zeros_like(acc)
        wvec[...] = jnp.zeros_like(wvec)

    sources = acc.shape[0]
    part = stores[0].shape[0]
    labels = lax.broadcasted_iota(jnp.int32, (sources, part), 0)
    for i, store in enumerate(stores):
        onehot = jnp.where(labels == ids[:, i * part : (i + 1) * part], 1.0, 0.0)
        acc[...] += jnp.dot(
            onehot.astype(jnp.bfloat16), store[...], preferred_element_type=jnp.float32
        )
    for i, down in enumerate(downs):
        wvec[i] += lax.dot_general(
            readout[...], down[...], CONTRACT, preferred_element_type=jnp.float32
        )

    @pl.when(step == pl.num_programs(0) - 1)
    def _():
        high = acc[...].astype(jnp.bfloat16)
        table[:sources, :] = high
        table[sources:, :] = (acc[...] - high.astype(jnp.float32)).astype(jnp.bfloat16)


def prepare(store, source_ids, down_weight, readout):
    examples, width = store.shape
    features, depth = down_weight.shape
    steps = 8
    block, deep = examples // steps, depth // steps
    part, piece = block // SPLIT, features // SPLIT
    table, wvec = pl.pallas_call(
        prepare_kernel,
        grid=(steps,),
        in_specs=[
            pl.BlockSpec((1, block), lambda k: (0, k)),
            pl.BlockSpec((8, deep), lambda k: (0, k)),
        ]
        + [pl.BlockSpec((part, width), lambda k, i=i: (k * SPLIT + i, 0)) for i in range(SPLIT)]
        + [pl.BlockSpec((piece, deep), lambda k, i=i: (i, k)) for i in range(SPLIT)],
        out_specs=[
            pl.BlockSpec((2 * SOURCES, width), lambda k: (0, 0)),
            pl.BlockSpec((SPLIT, 8, piece), lambda k: (0, 0, 0)),
        ],
        out_shape=[
            jax.ShapeDtypeStruct((2 * SOURCES, width), jnp.bfloat16),
            jax.ShapeDtypeStruct((SPLIT, 8, piece), jnp.float32),
        ],
        scratch_shapes=[pltpu.VMEM((SOURCES, width), jnp.float32)],
        compiler_params=pltpu.CompilerParams(vmem_limit_bytes=60 * 1024 * 1024),
        cost_estimate=pl.CostEstimate(
            flops=2 * SOURCES * examples * width,
            bytes_accessed=2 * examples * width + 2 * features * depth,
            transcendentals=0,
        ),
    )(
        source_ids.reshape(1, -1),
        jnp.broadcast_to(readout[None, :], (8, depth)),
        *[store] * SPLIT,
        *[down_weight] * SPLIT,
    )
    return table, wvec[:, 0].reshape(1, features)


def add_logit(sketch, logit, parts):
    rows = sketch.shape[0]
    wide = jnp.broadcast_to(logit[:, None, None], (rows, parts, 128))
    return jnp.concatenate([sketch.reshape(rows, parts, -1), wide], axis=2)


def sibling(value):
    return swap(value, "core", 1)


def plane_perm(masks):
    parts = lax.axis_size("pd")
    return [
        (core * parts + pd, core * parts + (pd ^ masks[core]))
        for core in range(CORES)
        for pd in range(parts)
    ]


def pack(sketch, logit):
    high = logit.astype(jnp.bfloat16)
    low = (logit - high.astype(jnp.float32)).astype(jnp.bfloat16)
    return jnp.concatenate([sketch.astype(jnp.bfloat16), high, low], axis=-1)


def add_packed(sketch, logit, packed):
    width, lanes = sketch.shape[-1], logit.shape[-1]
    high, low = packed[..., width : width + lanes], packed[..., width + lanes :]
    return (
        sketch + packed[..., :width].astype(jnp.float32),
        logit + (high.astype(jnp.float32) + low.astype(jnp.float32)),
    )


def ring_order(rows):
    parts, chips = lax.axis_size("pd"), lax.axis_size("chip")
    place, core = lax.axis_index("chip"), lax.axis_index("core")
    per = rows // (CORES * chips)
    row = jnp.arange(rows)
    at_layer, at_core, at = row // (CORES * per), row // per % CORES, row % per
    return ((at_core != core) * chips + (place - at_layer) % chips) * per + at


def piped_sketches(
    states, gate_weight, up_weight, wvec, table, sketch_in, sketch_out, rows, length, extras
):
    parts, chips = lax.axis_size("pd"), lax.axis_size("chip")
    place, core, pd = lax.axis_index("chip"), lax.axis_index("core"), lax.axis_index("pd")
    mine = states.shape[0]
    kin, kout = sketch_in.shape[0], sketch_out.shape[0]
    first, second = (2, 1), (1, 2)
    plane = ("core", "pd")
    tie = lax.optimization_barrier

    def send_a(value):
        return lax.ppermute(value, plane, plane_perm(first))

    def send_b(value):
        return lax.ppermute(value, plane, plane_perm(second))

    def ring(value, shift=1):
        return turn(value, "chip", shift)

    sin = sketch_in.reshape(parts, kin // parts, -1)[jnp.arange(parts) ^ pd]
    sin = sin.reshape(sketch_in.shape)

    def run(*pieces):
        return layer(pieces, gate_weight, up_weight, sin, sketch_out, wvec, length)

    p0 = states
    p0s = sibling(p0)
    a0, b0, p1 = send_a(p0), send_b(p0), ring(p0)
    a0, b0, table, wvec, sin = tie((a0, b0, table, wvec, sin))
    a0, p0 = tie((a0, p0))
    p3 = ring(p0, -1)
    a0s, b0s = sibling(a0), sibling(b0)
    a1, b1 = send_a(p1), send_b(p1)
    d0 = send_b(a0)
    out0 = run(p0, p0s, a0, a0s, b0, b0s)
    extras = extras(out0[1])
    p1s = sibling(p1)
    p1, p3, out0 = tie((p1, p3, out0))
    a1, b1, d0, out0 = tie((a1, b1, d0, out0))
    a3, b3, p2 = send_a(p3), send_b(p3), ring(p1)
    a1s, b1s, d0s = sibling(a1), sibling(b1), sibling(d0)
    d1 = send_b(a1)
    d0s, extras = tie((d0s, extras))
    out1 = run(d0, d0s, p1, p1s, a1, a1s, b1, b1s)
    p3s = sibling(p3)
    a3, b3, d1, p2, out1 = tie((a3, b3, d1, p2, out1))
    a2, b2, d2 = send_a(p2), send_b(p2), ring(d1)
    d3 = send_b(a3)
    a3s, b3s, d1s = sibling(a3), sibling(b3), sibling(d1)
    out2 = run(d1, d1s, p3, p3s, a3, a3s, b3, b3s)
    p2s = sibling(p2)
    a2, b2, d2, d3, out2 = tie((a2, b2, d2, d3, out2))
    out3 = run(
        d3, sibling(d3), p2, p2s, a2, sibling(a2), b2, sibling(b2), d2, sibling(d2)
    )
    outs = (out0, out1, out2, out3)
    place_of = jnp.array([0, 1, 3, 2])

    cores = (core + jnp.arange(CORES)) % CORES
    apart = jnp.arange(parts)[None, :] ^ pd
    is_a = jnp.where(cores[:, None] == 0, apart == first[0], apart == first[1])
    slot = jnp.where(apart == 0, 0, jnp.where(apart == 3, 6, jnp.where(is_a, 2, 4)))
    slot = slot + jnp.arange(CORES)[:, None]
    order = slot[:, None, :] + 2 * parts * place_of[None, :, None]
    order = order.reshape(-1)
    pieces = order.shape[0]
    proj = jnp.concatenate([o[0] for o in outs]).reshape(pieces, -1, kin + kout)[order]
    logit = jnp.concatenate([o[1] for o in outs]).reshape(pieces, -1, 8 * 128).sum(axis=2)[order]
    proj = proj.reshape(rows, length, kin + kout)
    sketch = jnp.einsum(
        "rti,rto->rio", proj[:, :, :kin], proj[:, :, kin:], precision=lax.Precision.HIGHEST
    )
    part = add_logit(sketch.reshape(rows, kin * kout), logit.reshape(rows), parts)
    half = part[: rows // CORES] + sibling(part[rows // CORES :])
    width = half.shape[2] - 128
    sketch, logit = half[:, 0, :width], half[:, 0, width : width + 64]
    for k in range(1, parts):
        packed = pack(half[:, k, :width], half[:, k, width : width + 64])
        sketch, logit = add_packed(sketch, logit, swap(packed, "pd", k))
    sketch, logit = (v.reshape(chips, -1, v.shape[1]) for v in (sketch, logit))
    packed = pack(sketch, logit)
    for k in range(1, chips):
        sketch, logit = add_packed(sketch, logit, jnp.roll(ring(packed, k), k, axis=0))
    whole = jnp.concatenate([sketch, logit, logit], axis=-1).reshape(rows // CORES, -1)
    both = jnp.concatenate([whole, sibling(whole)])
    return both, table, extras


def contrast_kernel(with_table, diff, *refs):
    step = pl.program_id(0)
    lead = 1 if with_table else 0
    table, stores, outs = refs[:lead], refs[lead : lead + SPLIT], refs[lead + SPLIT :]
    mine = outs[0].shape[0]

    if with_table:

        @pl.when(step == 0)
        def _():
            both = lax.dot_general(
                table[0][...], diff[...], CONTRACT, preferred_element_type=jnp.float32
            ).T
            half = both.shape[1] // 2
            score = both[:, :half] + both[:, half:]
            high = score.astype(jnp.bfloat16)
            low = (score - high.astype(jnp.float32)).astype(jnp.bfloat16)
            for i, out in enumerate(outs):
                out[:, :half] = high[i * mine : (i + 1) * mine]
                out[:, half:] = low[i * mine : (i + 1) * mine]

    @pl.when(step >= lead)
    def _():
        for j, store in enumerate(stores):
            part = lax.dot_general(
                store[...], diff[...], CONTRACT, preferred_element_type=jnp.float32
            ).T
            size = part.shape[1]
            for i, out in enumerate(outs):
                out[:, j * size : (j + 1) * size] = part[i * mine : (i + 1) * mine].astype(
                    out.dtype
                )


def contrast_parts(diff, store, first, blocks, parts, table=None):
    rows, width = diff.shape
    block = 2 * SOURCES
    lead = 0 if table is None else 1
    mine = rows // parts
    columns = block * (blocks + lead)
    tables = [] if table is None else [table]

    def stored(i):
        return pl.BlockSpec(
            (block // SPLIT, width),
            lambda k: ((first + jnp.maximum(k - lead, 0)) * SPLIT + i, 0),
        )

    return pl.pallas_call(
        functools.partial(contrast_kernel, table is not None),
        grid=(blocks + lead,),
        in_specs=[pl.BlockSpec((rows, width), lambda k: (0, 0))]
        + [pl.BlockSpec((block, width), lambda k: (0, 0))] * lead
        + [stored(i) for i in range(SPLIT)],
        out_specs=[pl.BlockSpec((mine, block), lambda k: (0, k))] * parts,
        out_shape=[jax.ShapeDtypeStruct((mine, columns), jnp.bfloat16)] * parts,
        compiler_params=pltpu.CompilerParams(vmem_limit_bytes=60 * 1024 * 1024),
        cost_estimate=pl.CostEstimate(
            flops=2 * rows * width * columns,
            bytes_accessed=2 * (width + rows) * columns,
            transcendentals=0,
        ),
    )(diff, *tables, *[store] * SPLIT)


def exchange(blocks):
    total = blocks[0].astype(jnp.float32)
    for k in range(1, len(blocks)):
        total = total + swap(blocks[k], "pd", k).astype(jnp.float32)
    return total


def plain_sketches(
    states, gate_weight, up_weight, wvec, table, sketch_in, sketch_out, rows, length, extras
):
    kin, kout = sketch_in.shape[0], sketch_out.shape[0]
    ff_local = gate_weight.shape[1]
    states = lax.all_gather(states, ("chip", "core", "pd"), axis=0, tiled=True)
    gate = jnp.dot(states, gate_weight, preferred_element_type=jnp.float32)
    up = jnp.dot(states, up_weight, preferred_element_type=jnp.float32)
    ain = lax.dot_general(states, sketch_in, CONTRACT, preferred_element_type=jnp.float32)
    sig = jax.nn.sigmoid(gate)
    weighted = up * wvec
    logit = jnp.sum((gate * sig * weighted).reshape(rows, length * ff_local), axis=1)
    dgate = (weighted * sig * (1.0 + gate * (1.0 - sig))).astype(jnp.bfloat16)
    bout = lax.dot_general(dgate, sketch_out, CONTRACT, preferred_element_type=jnp.float32)
    sketch = jnp.einsum(
        "rti,rto->rio",
        ain.reshape(rows, length, kin),
        bout.reshape(rows, length, kout),
        precision=lax.Precision.HIGHEST,
    ).reshape(rows, kin * kout)
    reduced = reduce_rows(add_logit(sketch, logit, lax.axis_size("pd")))
    return reduced, table, extras(reduced)


def on_device(
    verdict_states,
    verdict_labels,
    partner,
    gate_weight,
    up_weight,
    down_weight,
    readout,
    sketch_in,
    sketch_out,
    store,
    source_ids,
):
    rows = verdict_labels.shape[0]
    parts, chips = lax.axis_size("pd"), lax.axis_size("chip")
    pd = lax.axis_index("pd")
    examples, width = store.shape
    mine = verdict_states.shape[0]
    length = mine * parts * CORES * chips // rows

    table, wvec = prepare(store, source_ids, down_weight, readout)
    piped = (
        parts == 4
        and chips == 4
        and mine == 2 * length
        and length == 32
        and gate_weight.shape[1] % 128 == 0
        and gate_weight.shape[0] % 2048 == 0
        and gate_weight.shape[0] >= 6144
    )
    sketches = piped_sketches if piped else plain_sketches
    index = ring_order(rows) if piped else jnp.arange(rows)
    group = rows // parts

    def extras(after):
        mates, labels, _ = lax.optimization_barrier((partner, verdict_labels, after))
        order = jnp.concatenate([(pd ^ k) * group + jnp.arange(group) for k in range(parts)])
        labels = jnp.zeros_like(labels).at[index].set(labels)
        return 2.0 * labels.astype(jnp.float32) - 1.0, index[order], index[mates[order]]

    reduced, table, extras = sketches(
        verdict_states,
        gate_weight,
        up_weight,
        wvec,
        table,
        sketch_in,
        sketch_out,
        rows,
        length,
        extras,
    )
    sign, mine_at, mate_at = extras

    coef = -sign * jax.nn.sigmoid(-sign * (reduced[:, width] / length))
    scaled = reduced[:, :width] * (coef / length)[:, None]
    diff = (scaled[mine_at] - scaled[mate_at]).astype(jnp.bfloat16)

    blocks = examples // (2 * SOURCES)
    early = blocks // 2
    front = exchange(contrast_parts(diff, store, 0, early, parts, table))
    back = exchange(contrast_parts(diff, store, early, blocks - early, parts))
    scores = front[:, :SOURCES] + front[:, SOURCES : 2 * SOURCES]
    whole = scores
    for k in range(1, chips):
        whole = whole + turn(scores, "chip", k)
    whole = whole + sibling(whole)
    factor = (SOURCES / (examples * CORES * chips)) ** 0.5
    contrast = jnp.concatenate([front[:, 2 * SOURCES :], back], axis=1)
    return (contrast, whole * factor)


def solution(mesh):
    ex, pd = mesh.shape["ex"], mesh.shape["pd"]
    axed = Mesh(mesh.devices.reshape(ex // CORES, CORES, pd), ("chip", "core", "pd"))
    every = ("chip", "core", "pd")
    in_specs = (
        P(every, None),
        P(),
        P(),
        P(None, every),
        P(None, every),
        P(every, None),
        P(),
        P(),
        P(None, every),
        P(("chip", "core"), "pd"),
        P(("chip", "core")),
    )
    out_specs = (P("pd", ("chip", "core")), P("pd", None))
    return jax.shard_map(
        on_device, mesh=axed, in_specs=in_specs, out_specs=out_specs, check_vma=False
    )
```

```python
import functools

import jax
import jax.numpy as jnp
from jax import lax
from jax.experimental import pallas as pl
from jax.experimental.pallas import tpu as pltpu
from jax.sharding import Mesh
from jax.sharding import PartitionSpec as P

SOURCES = 512
CORES = 2
SPLIT = 4
CONTRACT = (((1,), (1,)), ((), ()))


def swap(value, axis, mask):
    size = lax.axis_size(axis)
    return lax.ppermute(value, axis, [(i, i ^ mask) for i in range(size)])


def turn(value, axis, shift):
    size = lax.axis_size(axis)
    return lax.ppermute(value, axis, [(i, (i + shift) % size) for i in range(size)])


def pick(value, index, axis):
    return lax.dynamic_index_in_dim(value, index, axis, keepdims=False)


def reduce_rows(part):
    rows, parts, width = part.shape
    core, pd = lax.axis_index("core"), lax.axis_index("pd")
    halves = part.reshape(CORES, rows // CORES, parts, width)
    half = pick(halves, core, 0) + swap(pick(halves, 1 - core, 0), "core", 1)
    total = pick(half, pd, 1)
    for k in range(1, parts):
        total = total + swap(pick(half, pd ^ k, 1), "pd", k)
    whole = total
    for k in range(1, lax.axis_size("chip")):
        whole = whole + turn(total, "chip", k)
    other = swap(whole, "core", 1)
    first = jnp.where(core == 0, whole, other)
    second = jnp.where(core == 0, other, whole)
    return jnp.concatenate([first, second], axis=0)


def layer_kernel(count, length, *refs):
    pieces = refs[:count]
    gate_w, up_w, sin, sout, wvec, proj, lrow, x, w, acc, dgate, sems = refs[count:]
    step = pl.program_id(0)
    steps = pl.num_programs(0)
    block = x.shape[1]
    features = gate_w.shape[1]
    tokens = pieces[0].shape[0]
    kin = sin.shape[0]

    def copies(k):
        slot = lax.rem(k, 2)
        here = pl.ds(pl.multiple_of(k * block, block), block)
        return [
            pltpu.make_async_copy(
                weight.at[here, :],
                w.at[slot, :, pl.ds(i * features, features)],
                sems.at[slot, i],
            )
            for i, weight in enumerate((gate_w, up_w))
        ]

    @pl.when(step == 0)
    def _():
        for copy in copies(step):
            copy.start()
        acc[...] = jnp.zeros_like(acc)
        proj[...] = jnp.zeros_like(proj)

    @pl.when(step + 1 < steps)
    def _():
        for copy in copies(step + 1):
            copy.start()

    for i, piece in enumerate(pieces):
        x[i * tokens : (i + 1) * tokens, :] = piece[...]
    for copy in copies(step):
        copy.wait()
    proj[:, :kin] += lax.dot_general(x[...], sin[...], CONTRACT, preferred_element_type=jnp.float32)
    acc[...] += jnp.dot(x[...], w[lax.rem(step, 2)], preferred_element_type=jnp.float32)

    @pl.when(step == steps - 1)
    def _():
        @pl.loop(0, acc.shape[0] // length)
        def _(i):
            here = pl.ds(pl.multiple_of(i * length, length), length)
            total = jnp.zeros((length, 128), jnp.float32)
            for j in range(features // 128):
                at = slice(j * 128, (j + 1) * 128)
                gate = acc[here, at]
                weighted = acc[here, features + j * 128 : features + (j + 1) * 128] * wvec[:, at]
                sig = jax.nn.sigmoid(gate)
                swish = gate * sig
                total = total + swish * weighted
                dgate[here, at] = (weighted * (sig + swish * (1.0 - sig))).astype(jnp.bfloat16)
            lrow[pl.ds(pl.multiple_of(8 * i, 8), 8), :] = total.reshape(-1, 8, 128).sum(axis=0)

        proj[:, kin:] = lax.dot_general(
            dgate[...], sout[...], CONTRACT, preferred_element_type=jnp.float32
        )


def layer(pieces, gate_weight, up_weight, sketch_in, sketch_out, wvec, length):
    count = len(pieces)
    tokens, depth = pieces[0].shape
    total = count * tokens
    features = gate_weight.shape[1]
    kin, kout = sketch_in.shape[0], sketch_out.shape[0]
    rows = total // length
    block = min(1024, depth)
    return pl.pallas_call(
        functools.partial(layer_kernel, count, length),
        grid=(depth // block,),
        in_specs=[pl.BlockSpec((tokens, block), lambda k: (0, k))] * count
        + [
            pl.BlockSpec(memory_space=pl.ANY),
            pl.BlockSpec(memory_space=pl.ANY),
            pl.BlockSpec((kin, block), lambda k: (0, k)),
            pl.BlockSpec((kout, features), lambda k: (0, 0)),
            pl.BlockSpec((1, features), lambda k: (0, 0)),
        ],
        out_specs=[
            pl.BlockSpec((total, kin + kout), lambda k: (0, 0)),
            pl.BlockSpec((rows * 8, 128), lambda k: (0, 0)),
        ],
        out_shape=[
            jax.ShapeDtypeStruct((total, kin + kout), jnp.float32),
            jax.ShapeDtypeStruct((rows * 8, 128), jnp.float32),
        ],
        scratch_shapes=[
            pltpu.VMEM((total, block), jnp.bfloat16),
            pltpu.VMEM((2, block, 2 * features), jnp.bfloat16),
            pltpu.VMEM((total, 2 * features), jnp.float32),
            pltpu.VMEM((total, features), jnp.bfloat16),
            pltpu.SemaphoreType.DMA((2, 2)),
        ],
        compiler_params=pltpu.CompilerParams(vmem_limit_bytes=60 * 1024 * 1024),
        cost_estimate=pl.CostEstimate(
            flops=4 * total * depth * features,
            bytes_accessed=2 * depth * (2 * features + total),
            transcendentals=total * features,
        ),
    )(*pieces, gate_weight, up_weight, sketch_in, sketch_out, wvec)


def prepare_kernel(ids, readout, *refs):
    stores, downs = refs[:SPLIT], refs[SPLIT : 2 * SPLIT]
    table, wvec, acc = refs[2 * SPLIT :]
    step = pl.program_id(0)

    @pl.when(step == 0)
    def _():
        acc[...] = jnp.zeros_like(acc)
        wvec[...] = jnp.zeros_like(wvec)

    sources = acc.shape[0]
    part = stores[0].shape[0]
    labels = lax.broadcasted_iota(jnp.int32, (sources, part), 0)
    for i, store in enumerate(stores):
        onehot = jnp.where(labels == ids[:, i * part : (i + 1) * part], 1.0, 0.0)
        acc[...] += jnp.dot(
            onehot.astype(jnp.bfloat16), store[...], preferred_element_type=jnp.float32
        )
    for i, down in enumerate(downs):
        wvec[i] += lax.dot_general(
            readout[...], down[...], CONTRACT, preferred_element_type=jnp.float32
        )

    @pl.when(step == pl.num_programs(0) - 1)
    def _():
        high = acc[...].astype(jnp.bfloat16)
        table[:sources, :] = high
        table[sources:, :] = (acc[...] - high.astype(jnp.float32)).astype(jnp.bfloat16)


def prepare(store, source_ids, down_weight, readout):
    examples, width = store.shape
    features, depth = down_weight.shape
    steps = 8
    block, deep = examples // steps, depth // steps
    part, piece = block // SPLIT, features // SPLIT
    table, wvec = pl.pallas_call(
        prepare_kernel,
        grid=(steps,),
        in_specs=[
            pl.BlockSpec((1, block), lambda k: (0, k)),
            pl.BlockSpec((8, deep), lambda k: (0, k)),
        ]
        + [pl.BlockSpec((part, width), lambda k, i=i: (k * SPLIT + i, 0)) for i in range(SPLIT)]
        + [pl.BlockSpec((piece, deep), lambda k, i=i: (i, k)) for i in range(SPLIT)],
        out_specs=[
            pl.BlockSpec((2 * SOURCES, width), lambda k: (0, 0)),
            pl.BlockSpec((SPLIT, 8, piece), lambda k: (0, 0, 0)),
        ],
        out_shape=[
            jax.ShapeDtypeStruct((2 * SOURCES, width), jnp.bfloat16),
            jax.ShapeDtypeStruct((SPLIT, 8, piece), jnp.float32),
        ],
        scratch_shapes=[pltpu.VMEM((SOURCES, width), jnp.float32)],
        compiler_params=pltpu.CompilerParams(vmem_limit_bytes=60 * 1024 * 1024),
        cost_estimate=pl.CostEstimate(
            flops=2 * SOURCES * examples * width,
            bytes_accessed=2 * examples * width + 2 * features * depth,
            transcendentals=0,
        ),
    )(
        source_ids.reshape(1, -1),
        jnp.broadcast_to(readout[None, :], (8, depth)),
        *[store] * SPLIT,
        *[down_weight] * SPLIT,
    )
    return table, wvec[:, 0].reshape(1, features)


def add_logit(sketch, logit, parts):
    rows = sketch.shape[0]
    wide = jnp.broadcast_to(logit[:, None, None], (rows, parts, 128))
    return jnp.concatenate([sketch.reshape(rows, parts, -1), wide], axis=2)


def sibling(value):
    return swap(value, "core", 1)


def plane_perm(masks):
    parts = lax.axis_size("pd")
    return [
        (core * parts + pd, core * parts + (pd ^ masks[core]))
        for core in range(CORES)
        for pd in range(parts)
    ]


def pack(sketch, logit):
    high = logit.astype(jnp.bfloat16)
    low = (logit - high.astype(jnp.float32)).astype(jnp.bfloat16)
    return jnp.concatenate([sketch.astype(jnp.bfloat16), high, low], axis=-1)


def add_packed(sketch, logit, packed):
    width, lanes = sketch.shape[-1], logit.shape[-1]
    high, low = packed[..., width : width + lanes], packed[..., width + lanes :]
    return (
        sketch + packed[..., :width].astype(jnp.float32),
        logit + (high.astype(jnp.float32) + low.astype(jnp.float32)),
    )


def ring_order(row, rows):
    chips = lax.axis_size("chip")
    place, core = lax.axis_index("chip"), lax.axis_index("core")
    per = rows // (CORES * chips)
    at_layer, at_core, at = row // (CORES * per), row // per % CORES, row % per
    return ((at_core != core) * chips + (place - at_layer) % chips) * per + at


def ring_rows(rows):
    chips = lax.axis_size("chip")
    place, core = lax.axis_index("chip"), lax.axis_index("core")
    per = rows // (CORES * chips)
    at = jnp.arange(rows)
    half, step = at // (chips * per), at // per % chips
    return ((place - step) % chips * CORES + (core ^ half)) * per + at % per


def piped_sketches(
    states, gate_weight, up_weight, wvec, table, sketch_in, sketch_out, rows, length, extras
):
    parts, chips = lax.axis_size("pd"), lax.axis_size("chip")
    place, core, pd = lax.axis_index("chip"), lax.axis_index("core"), lax.axis_index("pd")
    mine = states.shape[0]
    kin, kout = sketch_in.shape[0], sketch_out.shape[0]
    first, second = (2, 1), (1, 2)
    plane = ("core", "pd")
    tie = lax.optimization_barrier

    def send_a(value):
        return lax.ppermute(value, plane, plane_perm(first))

    def send_b(value):
        return lax.ppermute(value, plane, plane_perm(second))

    def ring(value, shift=1):
        return turn(value, "chip", shift)

    sin = sketch_in.reshape(parts, kin // parts, -1)[jnp.arange(parts) ^ pd]
    sin = sin.reshape(sketch_in.shape)

    def run(*pieces):
        return layer(pieces, gate_weight, up_weight, sin, sketch_out, wvec, length)

    p0 = states
    p0s = sibling(p0)
    a0, b0, p1 = send_a(p0), send_b(p0), ring(p0)
    a0, b0, table, wvec, sin = tie((a0, b0, table, wvec, sin))
    a0, p0 = tie((a0, p0))
    p3 = ring(p0, -1)
    a0s, b0s = sibling(a0), sibling(b0)
    a1, b1 = send_a(p1), send_b(p1)
    d0 = send_b(a0)
    out0 = run(p0, p0s, a0, a0s, b0, b0s)
    extras = extras(out0[1])
    p1s = sibling(p1)
    p1, p3, out0 = tie((p1, p3, out0))
    a1, b1, d0, out0 = tie((a1, b1, d0, out0))
    a3, b3, p2 = send_a(p3), send_b(p3), ring(p1)
    a1s, b1s, d0s = sibling(a1), sibling(b1), sibling(d0)
    d1 = send_b(a1)
    d0s, extras = tie((d0s, extras))
    out1 = run(d0, d0s, p1, p1s, a1, a1s, b1, b1s)
    p3s = sibling(p3)
    a3, b3, d1, p2, out1 = tie((a3, b3, d1, p2, out1))
    a2, b2, d2 = send_a(p2), send_b(p2), ring(d1)
    d3 = send_b(a3)
    a3s, b3s, d1s = sibling(a3), sibling(b3), sibling(d1)
    out2 = run(d1, d1s, p3, p3s, a3, a3s, b3, b3s)
    p2s = sibling(p2)
    a2, b2, d2, d3, out2 = tie((a2, b2, d2, d3, out2))
    out3 = run(
        d3, sibling(d3), p2, p2s, a2, sibling(a2), b2, sibling(b2), d2, sibling(d2)
    )
    outs = (out0, out1, out2, out3)
    place_of = jnp.array([0, 1, 3, 2])

    cores = (core + jnp.arange(CORES)) % CORES
    apart = jnp.arange(parts)[None, :] ^ pd
    is_a = jnp.where(cores[:, None] == 0, apart == first[0], apart == first[1])
    slot = jnp.where(apart == 0, 0, jnp.where(apart == 3, 6, jnp.where(is_a, 2, 4)))
    slot = slot + jnp.arange(CORES)[:, None]
    order = slot[:, None, :] + 2 * parts * place_of[None, :, None]
    order = order.reshape(-1)
    pieces = order.shape[0]
    proj = jnp.concatenate([o[0] for o in outs]).reshape(pieces, -1, kin + kout)[order]
    logit = jnp.concatenate([o[1] for o in outs]).reshape(pieces, -1, 8 * 128).sum(axis=2)[order]
    proj = proj.reshape(rows, length, kin + kout)
    sketch = jnp.einsum(
        "rti,rto->rio", proj[:, :, :kin], proj[:, :, kin:], precision=lax.Precision.HIGH
    ).reshape(rows, kin * kout)
    wide = jnp.broadcast_to(logit.reshape(rows, 1), (rows, 128))
    part = jnp.concatenate([sketch, wide], axis=1)
    half = part[: rows // CORES] + sibling(part[rows // CORES :])
    width = kin * kout // parts
    blocks = [half[:, k * width : (k + 1) * width] for k in range(parts)]
    lanes = half[:, kin * kout : kin * kout + 64]
    sketch, logit = blocks[0], lanes
    for k in range(1, parts):
        sketch, logit = add_packed(sketch, logit, swap(pack(blocks[k], lanes), "pd", k))
    sketch, logit = (v.reshape(chips, -1, v.shape[1]) for v in (sketch, logit))
    packed = pack(sketch, logit)
    for k in range(1, chips):
        sketch, logit = add_packed(sketch, logit, jnp.roll(ring(packed, k), k, axis=0))
    whole = jnp.concatenate([sketch, logit, logit], axis=-1).reshape(rows // CORES, -1)
    both = jnp.concatenate([whole, sibling(whole)])
    return both, table, extras


def contrast_kernel(with_table, diff, *refs):
    step = pl.program_id(0)
    lead = 1 if with_table else 0
    table, stores, outs = refs[:lead], refs[lead : lead + SPLIT], refs[lead + SPLIT :]
    mine = outs[0].shape[0]

    if with_table:

        @pl.when(step == 0)
        def _():
            both = lax.dot_general(
                table[0][...], diff[...], CONTRACT, preferred_element_type=jnp.float32
            ).T
            half = both.shape[1] // 2
            score = both[:, :half] + both[:, half:]
            high = score.astype(jnp.bfloat16)
            low = (score - high.astype(jnp.float32)).astype(jnp.bfloat16)
            for i, out in enumerate(outs):
                out[:, :half] = high[i * mine : (i + 1) * mine]
                out[:, half:] = low[i * mine : (i + 1) * mine]

    @pl.when(step >= lead)
    def _():
        for j, store in enumerate(stores):
            part = lax.dot_general(
                store[...], diff[...], CONTRACT, preferred_element_type=jnp.float32
            ).T
            size = part.shape[1]
            for i, out in enumerate(outs):
                out[:, j * size : (j + 1) * size] = part[i * mine : (i + 1) * mine].astype(
                    out.dtype
                )


def contrast_parts(diff, store, first, blocks, parts, table=None):
    rows, width = diff.shape
    block = 2 * SOURCES
    lead = 0 if table is None else 1
    mine = rows // parts
    columns = block * (blocks + lead)
    tables = [] if table is None else [table]

    def stored(i):
        return pl.BlockSpec(
            (block // SPLIT, width),
            lambda k: ((first + jnp.maximum(k - lead, 0)) * SPLIT + i, 0),
        )

    return pl.pallas_call(
        functools.partial(contrast_kernel, table is not None),
        grid=(blocks + lead,),
        in_specs=[pl.BlockSpec((rows, width), lambda k: (0, 0))]
        + [pl.BlockSpec((block, width), lambda k: (0, 0))] * lead
        + [stored(i) for i in range(SPLIT)],
        out_specs=[pl.BlockSpec((mine, block), lambda k: (0, k))] * parts,
        out_shape=[jax.ShapeDtypeStruct((mine, columns), jnp.bfloat16)] * parts,
        compiler_params=pltpu.CompilerParams(vmem_limit_bytes=60 * 1024 * 1024),
        cost_estimate=pl.CostEstimate(
            flops=2 * rows * width * columns,
            bytes_accessed=2 * (width + rows) * columns,
            transcendentals=0,
        ),
    )(diff, *tables, *[store] * SPLIT)


def exchange(blocks):
    total = blocks[0].astype(jnp.float32)
    for k in range(1, len(blocks)):
        total = total + swap(blocks[k], "pd", k).astype(jnp.float32)
    return total


def plain_sketches(
    states, gate_weight, up_weight, wvec, table, sketch_in, sketch_out, rows, length, extras
):
    kin, kout = sketch_in.shape[0], sketch_out.shape[0]
    ff_local = gate_weight.shape[1]
    states = lax.all_gather(states, ("chip", "core", "pd"), axis=0, tiled=True)
    gate = jnp.dot(states, gate_weight, preferred_element_type=jnp.float32)
    up = jnp.dot(states, up_weight, preferred_element_type=jnp.float32)
    ain = lax.dot_general(states, sketch_in, CONTRACT, preferred_element_type=jnp.float32)
    sig = jax.nn.sigmoid(gate)
    weighted = up * wvec
    logit = jnp.sum((gate * sig * weighted).reshape(rows, length * ff_local), axis=1)
    dgate = (weighted * sig * (1.0 + gate * (1.0 - sig))).astype(jnp.bfloat16)
    bout = lax.dot_general(dgate, sketch_out, CONTRACT, preferred_element_type=jnp.float32)
    sketch = jnp.einsum(
        "rti,rto->rio",
        ain.reshape(rows, length, kin),
        bout.reshape(rows, length, kout),
        precision=lax.Precision.HIGHEST,
    ).reshape(rows, kin * kout)
    reduced = reduce_rows(add_logit(sketch, logit, lax.axis_size("pd")))
    return reduced, table, extras(reduced)


def on_device(
    verdict_states,
    verdict_labels,
    partner,
    gate_weight,
    up_weight,
    down_weight,
    readout,
    sketch_in,
    sketch_out,
    store,
    source_ids,
):
    rows = verdict_labels.shape[0]
    parts, chips = lax.axis_size("pd"), lax.axis_size("chip")
    pd = lax.axis_index("pd")
    examples, width = store.shape
    mine = verdict_states.shape[0]
    length = mine * parts * CORES * chips // rows

    table, wvec = prepare(store, source_ids, down_weight, readout)
    piped = (
        parts == 4
        and chips == 4
        and mine == 2 * length
        and length == 32
        and gate_weight.shape[1] % 128 == 0
        and gate_weight.shape[0] % 2048 == 0
        and gate_weight.shape[0] >= 6144
    )
    sketches = piped_sketches if piped else plain_sketches
    group = rows // parts

    def extras(after):
        mates, labels, _ = lax.optimization_barrier((partner, verdict_labels, after))
        order = jnp.concatenate([(pd ^ k) * group + jnp.arange(group) for k in range(parts)])
        own, mate = order, mates[order]
        if piped:
            labels = labels[ring_rows(rows)]
            own, mate = ring_order(own, rows), ring_order(mate, rows)
        return 2.0 * labels.astype(jnp.float32) - 1.0, own, mate

    reduced, table, extras = sketches(
        verdict_states,
        gate_weight,
        up_weight,
        wvec,
        table,
        sketch_in,
        sketch_out,
        rows,
        length,
        extras,
    )
    sign, mine_at, mate_at = extras

    coef = -sign * jax.nn.sigmoid(-sign * (reduced[:, width] / length))
    scaled = reduced[:, :width] * (coef / length)[:, None]
    diff = (scaled[mine_at] - scaled[mate_at]).astype(jnp.bfloat16)

    blocks = examples // (2 * SOURCES)
    early = blocks // 2
    front = exchange(contrast_parts(diff, store, 0, early, parts, table))
    back = exchange(contrast_parts(diff, store, early, blocks - early, parts))
    scores = front[:, :SOURCES] + front[:, SOURCES : 2 * SOURCES]
    whole = scores
    for k in range(1, chips):
        whole = whole + turn(scores, "chip", k)
    whole = whole + sibling(whole)
    factor = (SOURCES / (examples * CORES * chips)) ** 0.5
    contrast = jnp.concatenate([front[:, 2 * SOURCES :], back], axis=1)
    return (contrast, whole * factor)


def solution(mesh):
    ex, pd = mesh.shape["ex"], mesh.shape["pd"]
    axed = Mesh(mesh.devices.reshape(ex // CORES, CORES, pd), ("chip", "core", "pd"))
    every = ("chip", "core", "pd")
    in_specs = (
        P(every, None),
        P(),
        P(),
        P(None, every),
        P(None, every),
        P(every, None),
        P(),
        P(),
        P(None, every),
        P(("chip", "core"), "pd"),
        P(("chip", "core")),
    )
    out_specs = (P("pd", ("chip", "core")), P("pd", None))
    return jax.shard_map(
        on_device, mesh=axed, in_specs=in_specs, out_specs=out_specs, check_vma=False
    )
```

```python
import functools

import jax
import jax.numpy as jnp
from jax import lax
from jax.experimental import pallas as pl
from jax.experimental.pallas import tpu as pltpu
from jax.sharding import Mesh
from jax.sharding import PartitionSpec as P

SOURCES = 512
CORES = 2
SPLIT = 4
CONTRACT = (((1,), (1,)), ((), ()))


def swap(value, axis, mask):
    size = lax.axis_size(axis)
    return lax.ppermute(value, axis, [(i, i ^ mask) for i in range(size)])


def turn(value, axis, shift):
    size = lax.axis_size(axis)
    return lax.ppermute(value, axis, [(i, (i + shift) % size) for i in range(size)])


def pick(value, index, axis):
    return lax.dynamic_index_in_dim(value, index, axis, keepdims=False)


def reduce_rows(part):
    rows, parts, width = part.shape
    core, pd = lax.axis_index("core"), lax.axis_index("pd")
    halves = part.reshape(CORES, rows // CORES, parts, width)
    half = pick(halves, core, 0) + swap(pick(halves, 1 - core, 0), "core", 1)
    total = pick(half, pd, 1)
    for k in range(1, parts):
        total = total + swap(pick(half, pd ^ k, 1), "pd", k)
    whole = total
    for k in range(1, lax.axis_size("chip")):
        whole = whole + turn(total, "chip", k)
    other = swap(whole, "core", 1)
    first = jnp.where(core == 0, whole, other)
    second = jnp.where(core == 0, other, whole)
    return jnp.concatenate([first, second], axis=0)


def layer_kernel(count, length, *refs):
    pieces = refs[:count]
    gate_w, up_w, sin, sout, wvec, proj, lrow, x, w, acc, dgate, sems = refs[count:]
    step = pl.program_id(0)
    steps = pl.num_programs(0)
    block = x.shape[1]
    features = gate_w.shape[1]
    tokens = pieces[0].shape[0]
    kin = sin.shape[0]

    def copies(k):
        slot = lax.rem(k, 2)
        here = pl.ds(pl.multiple_of(k * block, block), block)
        return [
            pltpu.make_async_copy(
                weight.at[here, :],
                w.at[slot, :, pl.ds(i * features, features)],
                sems.at[slot, i],
            )
            for i, weight in enumerate((gate_w, up_w))
        ]

    @pl.when(step == 0)
    def _():
        for copy in copies(step):
            copy.start()
        acc[...] = jnp.zeros_like(acc)
        proj[...] = jnp.zeros_like(proj)

    @pl.when(step + 1 < steps)
    def _():
        for copy in copies(step + 1):
            copy.start()

    for i, piece in enumerate(pieces):
        x[i * tokens : (i + 1) * tokens, :] = piece[...]
    for copy in copies(step):
        copy.wait()
    proj[:, :kin] += lax.dot_general(x[...], sin[...], CONTRACT, preferred_element_type=jnp.float32)
    acc[...] += jnp.dot(x[...], w[lax.rem(step, 2)], preferred_element_type=jnp.float32)

    @pl.when(step == steps - 1)
    def _():
        @pl.loop(0, acc.shape[0] // length)
        def _(i):
            here = pl.ds(pl.multiple_of(i * length, length), length)
            total = jnp.zeros((length, 128), jnp.float32)
            for j in range(features // 128):
                at = slice(j * 128, (j + 1) * 128)
                gate = acc[here, at]
                weighted = acc[here, features + j * 128 : features + (j + 1) * 128] * wvec[:, at]
                sig = jax.nn.sigmoid(gate)
                swish = gate * sig
                total = total + swish * weighted
                dgate[here, at] = (weighted * (sig + swish * (1.0 - sig))).astype(jnp.bfloat16)
            lrow[pl.ds(pl.multiple_of(8 * i, 8), 8), :] = total.reshape(-1, 8, 128).sum(axis=0)

        proj[:, kin:] = lax.dot_general(
            dgate[...], sout[...], CONTRACT, preferred_element_type=jnp.float32
        )


def layer(pieces, gate_weight, up_weight, sketch_in, sketch_out, wvec, length):
    count = len(pieces)
    tokens, depth = pieces[0].shape
    total = count * tokens
    features = gate_weight.shape[1]
    kin, kout = sketch_in.shape[0], sketch_out.shape[0]
    rows = total // length
    block = min(1024, depth)
    return pl.pallas_call(
        functools.partial(layer_kernel, count, length),
        grid=(depth // block,),
        in_specs=[pl.BlockSpec((tokens, block), lambda k: (0, k))] * count
        + [
            pl.BlockSpec(memory_space=pl.ANY),
            pl.BlockSpec(memory_space=pl.ANY),
            pl.BlockSpec((kin, block), lambda k: (0, k)),
            pl.BlockSpec((kout, features), lambda k: (0, 0)),
            pl.BlockSpec((1, features), lambda k: (0, 0)),
        ],
        out_specs=[
            pl.BlockSpec((total, kin + kout), lambda k: (0, 0)),
            pl.BlockSpec((rows * 8, 128), lambda k: (0, 0)),
        ],
        out_shape=[
            jax.ShapeDtypeStruct((total, kin + kout), jnp.float32),
            jax.ShapeDtypeStruct((rows * 8, 128), jnp.float32),
        ],
        scratch_shapes=[
            pltpu.VMEM((total, block), jnp.bfloat16),
            pltpu.VMEM((2, block, 2 * features), jnp.bfloat16),
            pltpu.VMEM((total, 2 * features), jnp.float32),
            pltpu.VMEM((total, features), jnp.bfloat16),
            pltpu.SemaphoreType.DMA((2, 2)),
        ],
        compiler_params=pltpu.CompilerParams(vmem_limit_bytes=60 * 1024 * 1024),
        cost_estimate=pl.CostEstimate(
            flops=4 * total * depth * features,
            bytes_accessed=2 * depth * (2 * features + total),
            transcendentals=total * features,
        ),
    )(*pieces, gate_weight, up_weight, sketch_in, sketch_out, wvec)


def prepare_kernel(ids, readout, *refs):
    stores, downs = refs[:SPLIT], refs[SPLIT : 2 * SPLIT]
    table, wvec, acc = refs[2 * SPLIT :]
    step = pl.program_id(0)

    @pl.when(step == 0)
    def _():
        acc[...] = jnp.zeros_like(acc)
        wvec[...] = jnp.zeros_like(wvec)

    sources = acc.shape[0]
    part = stores[0].shape[0]
    labels = lax.broadcasted_iota(jnp.int32, (sources, part), 0)
    for i, store in enumerate(stores):
        onehot = jnp.where(labels == ids[:, i * part : (i + 1) * part], 1.0, 0.0)
        acc[...] += jnp.dot(
            onehot.astype(jnp.bfloat16), store[...], preferred_element_type=jnp.float32
        )
    for i, down in enumerate(downs):
        wvec[i] += lax.dot_general(
            readout[...], down[...], CONTRACT, preferred_element_type=jnp.float32
        )

    @pl.when(step == pl.num_programs(0) - 1)
    def _():
        high = acc[...].astype(jnp.bfloat16)
        table[:sources, :] = high
        table[sources:, :] = (acc[...] - high.astype(jnp.float32)).astype(jnp.bfloat16)


def prepare(store, source_ids, down_weight, readout):
    examples, width = store.shape
    features, depth = down_weight.shape
    steps = 8
    block, deep = examples // steps, depth // steps
    part, piece = block // SPLIT, features // SPLIT
    table, wvec = pl.pallas_call(
        prepare_kernel,
        grid=(steps,),
        in_specs=[
            pl.BlockSpec((1, block), lambda k: (0, k)),
            pl.BlockSpec((8, deep), lambda k: (0, k)),
        ]
        + [pl.BlockSpec((part, width), lambda k, i=i: (k * SPLIT + i, 0)) for i in range(SPLIT)]
        + [pl.BlockSpec((piece, deep), lambda k, i=i: (i, k)) for i in range(SPLIT)],
        out_specs=[
            pl.BlockSpec((2 * SOURCES, width), lambda k: (0, 0)),
            pl.BlockSpec((SPLIT, 8, piece), lambda k: (0, 0, 0)),
        ],
        out_shape=[
            jax.ShapeDtypeStruct((2 * SOURCES, width), jnp.bfloat16),
            jax.ShapeDtypeStruct((SPLIT, 8, piece), jnp.float32),
        ],
        scratch_shapes=[pltpu.VMEM((SOURCES, width), jnp.float32)],
        compiler_params=pltpu.CompilerParams(vmem_limit_bytes=60 * 1024 * 1024),
        cost_estimate=pl.CostEstimate(
            flops=2 * SOURCES * examples * width,
            bytes_accessed=2 * examples * width + 2 * features * depth,
            transcendentals=0,
        ),
    )(
        source_ids.reshape(1, -1),
        jnp.broadcast_to(readout[None, :], (8, depth)),
        *[store] * SPLIT,
        *[down_weight] * SPLIT,
    )
    return table, wvec[:, 0].reshape(1, features)


def add_logit(sketch, logit, parts):
    rows = sketch.shape[0]
    wide = jnp.broadcast_to(logit[:, None, None], (rows, parts, 128))
    return jnp.concatenate([sketch.reshape(rows, parts, -1), wide], axis=2)


def sibling(value):
    return swap(value, "core", 1)


def plane_perm(masks):
    parts = lax.axis_size("pd")
    return [
        (core * parts + pd, core * parts + (pd ^ masks[core]))
        for core in range(CORES)
        for pd in range(parts)
    ]


def pack(sketch, logit):
    high = logit.astype(jnp.bfloat16)
    low = (logit - high.astype(jnp.float32)).astype(jnp.bfloat16)
    return jnp.concatenate([sketch.astype(jnp.bfloat16), high, low], axis=-1)


def add_packed(sketch, logit, packed):
    width, lanes = sketch.shape[-1], logit.shape[-1]
    high, low = packed[..., width : width + lanes], packed[..., width + lanes :]
    return (
        sketch + packed[..., :width].astype(jnp.float32),
        logit + (high.astype(jnp.float32) + low.astype(jnp.float32)),
    )


def ring_order(row, rows):
    chips = lax.axis_size("chip")
    place, core = lax.axis_index("chip"), lax.axis_index("core")
    per = rows // (CORES * chips)
    at_layer, at_core, at = row // (CORES * per), row // per % CORES, row % per
    return ((at_core != core) * chips + (place - at_layer) % chips) * per + at


def ring_rows(rows):
    chips = lax.axis_size("chip")
    place, core = lax.axis_index("chip"), lax.axis_index("core")
    per = rows // (CORES * chips)
    at = jnp.arange(rows)
    half, step = at // (chips * per), at // per % chips
    return ((place - step) % chips * CORES + (core ^ half)) * per + at % per


def piped_sketches(
    states, gate_weight, up_weight, wvec, table, sketch_in, sketch_out, rows, length, extras
):
    parts, chips = lax.axis_size("pd"), lax.axis_size("chip")
    place, core, pd = lax.axis_index("chip"), lax.axis_index("core"), lax.axis_index("pd")
    mine = states.shape[0]
    kin, kout = sketch_in.shape[0], sketch_out.shape[0]
    first, second = (2, 1), (1, 2)
    plane = ("core", "pd")
    tie = lax.optimization_barrier

    def send_a(value):
        return lax.ppermute(value, plane, plane_perm(first))

    def send_b(value):
        return lax.ppermute(value, plane, plane_perm(second))

    def ring(value, shift=1):
        return turn(value, "chip", shift)

    def reorder(sketch_in):
        by_part = sketch_in.reshape(parts, kin // parts, -1)
        return by_part[jnp.arange(parts) ^ pd].reshape(sketch_in.shape)

    def run(*pieces):
        return layer(pieces, gate_weight, up_weight, sin, sketch_out, wvec, length)

    p0 = states
    p0s = sibling(p0)
    a0, b0, p1 = send_a(p0), send_b(p0), ring(p0)
    a0, b0, p1, table = tie((a0, b0, p1, table))
    a1, b1, d0 = send_a(p1), send_b(p1), send_b(a0)
    sketch_in, wvec, _ = tie((sketch_in, wvec, a0))
    sin = reorder(sketch_in)
    a0, p0 = tie((a0, p0))
    p3 = ring(p0, -1)
    a0s, b0s = sibling(a0), sibling(b0)
    out0 = run(p0, p0s, a0, a0s, b0, b0s)
    extras = extras(out0[1])
    p1s = sibling(p1)
    p1, p3, out0 = tie((p1, p3, out0))
    a1, b1, d0, out0 = tie((a1, b1, d0, out0))
    a3, b3, p2 = send_a(p3), send_b(p3), ring(p1)
    a1s, b1s, d0s = sibling(a1), sibling(b1), sibling(d0)
    d1 = send_b(a1)
    d0s, extras = tie((d0s, extras))
    out1 = run(d0, d0s, p1, p1s, a1, a1s, b1, b1s)
    p3s = sibling(p3)
    a3, b3, d1, p2, out1 = tie((a3, b3, d1, p2, out1))
    a2, b2, d2 = send_a(p2), send_b(p2), ring(d1)
    d3 = send_b(a3)
    a3s, b3s, d1s = sibling(a3), sibling(b3), sibling(d1)
    out2 = run(d1, d1s, p3, p3s, a3, a3s, b3, b3s)
    p2s = sibling(p2)
    a2, b2, d2, d3, out2 = tie((a2, b2, d2, d3, out2))
    out3 = run(
        d3, sibling(d3), p2, p2s, a2, sibling(a2), b2, sibling(b2), d2, sibling(d2)
    )
    outs = (out0, out1, out2, out3)
    place_of = jnp.array([0, 1, 3, 2])

    cores = (core + jnp.arange(CORES)) % CORES
    apart = jnp.arange(parts)[None, :] ^ pd
    is_a = jnp.where(cores[:, None] == 0, apart == first[0], apart == first[1])
    slot = jnp.where(apart == 0, 0, jnp.where(apart == 3, 6, jnp.where(is_a, 2, 4)))
    slot = slot + jnp.arange(CORES)[:, None]
    order = slot[:, None, :] + 2 * parts * place_of[None, :, None]
    order = order.reshape(-1)
    pieces = order.shape[0]
    proj = jnp.concatenate([o[0] for o in outs]).reshape(pieces, -1, kin + kout)[order]
    logit = jnp.concatenate([o[1] for o in outs]).reshape(pieces, -1, 8 * 128).sum(axis=2)[order]
    proj = proj.reshape(rows, length, kin + kout)
    sketch = jnp.einsum(
        "rti,rto->rio", proj[:, :, :kin], proj[:, :, kin:], precision=lax.Precision.HIGH
    ).reshape(rows, kin * kout)
    wide = jnp.broadcast_to(logit.reshape(rows, 1), (rows, 128))
    part = jnp.concatenate([sketch, wide], axis=1)
    half = part[: rows // CORES] + sibling(part[rows // CORES :])
    width = kin * kout // parts
    blocks = [half[:, k * width : (k + 1) * width] for k in range(parts)]
    lanes = half[:, kin * kout : kin * kout + 64]
    sketch, logit = blocks[0], lanes
    for k in range(1, parts):
        sketch, logit = add_packed(sketch, logit, swap(pack(blocks[k], lanes), "pd", k))
    sketch, logit = (v.reshape(chips, -1, v.shape[1]) for v in (sketch, logit))
    packed = pack(sketch, logit)
    for k in range(1, chips):
        sketch, logit = add_packed(sketch, logit, jnp.roll(ring(packed, k), k, axis=0))
    whole = jnp.concatenate([sketch, logit, logit], axis=-1).reshape(rows // CORES, -1)
    both = jnp.concatenate([whole, sibling(whole)])
    return both, table, extras


def contrast_kernel(with_table, diff, *refs):
    step = pl.program_id(0)
    lead = 1 if with_table else 0
    table, stores, outs = refs[:lead], refs[lead : lead + SPLIT], refs[lead + SPLIT :]
    mine = outs[0].shape[0]

    if with_table:

        @pl.when(step == 0)
        def _():
            both = lax.dot_general(
                table[0][...], diff[...], CONTRACT, preferred_element_type=jnp.float32
            ).T
            half = both.shape[1] // 2
            score = both[:, :half] + both[:, half:]
            high = score.astype(jnp.bfloat16)
            low = (score - high.astype(jnp.float32)).astype(jnp.bfloat16)
            for i, out in enumerate(outs):
                out[:, :half] = high[i * mine : (i + 1) * mine]
                out[:, half:] = low[i * mine : (i + 1) * mine]

    @pl.when(step >= lead)
    def _():
        for j, store in enumerate(stores):
            part = lax.dot_general(
                store[...], diff[...], CONTRACT, preferred_element_type=jnp.float32
            ).T
            size = part.shape[1]
            for i, out in enumerate(outs):
                out[:, j * size : (j + 1) * size] = part[i * mine : (i + 1) * mine].astype(
                    out.dtype
                )


def contrast_parts(diff, store, first, blocks, parts, table=None):
    rows, width = diff.shape
    block = 2 * SOURCES
    lead = 0 if table is None else 1
    mine = rows // parts
    columns = block * (blocks + lead)
    tables = [] if table is None else [table]

    def stored(i):
        return pl.BlockSpec(
            (block // SPLIT, width),
            lambda k: ((first + jnp.maximum(k - lead, 0)) * SPLIT + i, 0),
        )

    return pl.pallas_call(
        functools.partial(contrast_kernel, table is not None),
        grid=(blocks + lead,),
        in_specs=[pl.BlockSpec((rows, width), lambda k: (0, 0))]
        + [pl.BlockSpec((block, width), lambda k: (0, 0))] * lead
        + [stored(i) for i in range(SPLIT)],
        out_specs=[pl.BlockSpec((mine, block), lambda k: (0, k))] * parts,
        out_shape=[jax.ShapeDtypeStruct((mine, columns), jnp.bfloat16)] * parts,
        compiler_params=pltpu.CompilerParams(vmem_limit_bytes=60 * 1024 * 1024),
        cost_estimate=pl.CostEstimate(
            flops=2 * rows * width * columns,
            bytes_accessed=2 * (width + rows) * columns,
            transcendentals=0,
        ),
    )(diff, *tables, *[store] * SPLIT)


def exchange(blocks):
    total = blocks[0].astype(jnp.float32)
    for k in range(1, len(blocks)):
        total = total + swap(blocks[k], "pd", k).astype(jnp.float32)
    return total


def plain_sketches(
    states, gate_weight, up_weight, wvec, table, sketch_in, sketch_out, rows, length, extras
):
    kin, kout = sketch_in.shape[0], sketch_out.shape[0]
    ff_local = gate_weight.shape[1]
    states = lax.all_gather(states, ("chip", "core", "pd"), axis=0, tiled=True)
    gate = jnp.dot(states, gate_weight, preferred_element_type=jnp.float32)
    up = jnp.dot(states, up_weight, preferred_element_type=jnp.float32)
    ain = lax.dot_general(states, sketch_in, CONTRACT, preferred_element_type=jnp.float32)
    sig = jax.nn.sigmoid(gate)
    weighted = up * wvec
    logit = jnp.sum((gate * sig * weighted).reshape(rows, length * ff_local), axis=1)
    dgate = (weighted * sig * (1.0 + gate * (1.0 - sig))).astype(jnp.bfloat16)
    bout = lax.dot_general(dgate, sketch_out, CONTRACT, preferred_element_type=jnp.float32)
    sketch = jnp.einsum(
        "rti,rto->rio",
        ain.reshape(rows, length, kin),
        bout.reshape(rows, length, kout),
        precision=lax.Precision.HIGHEST,
    ).reshape(rows, kin * kout)
    reduced = reduce_rows(add_logit(sketch, logit, lax.axis_size("pd")))
    return reduced, table, extras(reduced)


def on_device(
    verdict_states,
    verdict_labels,
    partner,
    gate_weight,
    up_weight,
    down_weight,
    readout,
    sketch_in,
    sketch_out,
    store,
    source_ids,
):
    rows = verdict_labels.shape[0]
    parts, chips = lax.axis_size("pd"), lax.axis_size("chip")
    pd = lax.axis_index("pd")
    examples, width = store.shape
    mine = verdict_states.shape[0]
    length = mine * parts * CORES * chips // rows

    table, wvec = prepare(store, source_ids, down_weight, readout)
    piped = (
        parts == 4
        and chips == 4
        and mine == 2 * length
        and length == 32
        and gate_weight.shape[1] % 128 == 0
        and gate_weight.shape[0] % 2048 == 0
        and gate_weight.shape[0] >= 6144
    )
    sketches = piped_sketches if piped else plain_sketches
    group = rows // parts

    def extras(after):
        mates, labels, _ = lax.optimization_barrier((partner, verdict_labels, after))
        order = jnp.concatenate([(pd ^ k) * group + jnp.arange(group) for k in range(parts)])
        own, mate = order, mates[order]
        if piped:
            labels = labels[ring_rows(rows)]
            own, mate = ring_order(own, rows), ring_order(mate, rows)
        return 2.0 * labels.astype(jnp.float32) - 1.0, own, mate

    reduced, table, extras = sketches(
        verdict_states,
        gate_weight,
        up_weight,
        wvec,
        table,
        sketch_in,
        sketch_out,
        rows,
        length,
        extras,
    )
    sign, mine_at, mate_at = extras

    coef = -sign * jax.nn.sigmoid(-sign * (reduced[:, width] / length))
    scaled = reduced[:, :width] * (coef / length)[:, None]
    diff = (scaled[mine_at] - scaled[mate_at]).astype(jnp.bfloat16)

    blocks = examples // (2 * SOURCES)
    early = blocks // 2
    front = exchange(contrast_parts(diff, store, 0, early, parts, table))
    back = exchange(contrast_parts(diff, store, early, blocks - early, parts))
    scores = front[:, :SOURCES] + front[:, SOURCES : 2 * SOURCES]
    whole = scores
    for k in range(1, chips):
        whole = whole + turn(scores, "chip", k)
    whole = whole + sibling(whole)
    factor = (SOURCES / (examples * CORES * chips)) ** 0.5
    contrast = jnp.concatenate([front[:, 2 * SOURCES :], back], axis=1)
    return (contrast, whole * factor)


def solution(mesh):
    ex, pd = mesh.shape["ex"], mesh.shape["pd"]
    axed = Mesh(mesh.devices.reshape(ex // CORES, CORES, pd), ("chip", "core", "pd"))
    every = ("chip", "core", "pd")
    in_specs = (
        P(every, None),
        P(),
        P(),
        P(None, every),
        P(None, every),
        P(every, None),
        P(),
        P(),
        P(None, every),
        P(("chip", "core"), "pd"),
        P(("chip", "core")),
    )
    out_specs = (P("pd", ("chip", "core")), P("pd", None))
    return jax.shard_map(
        on_device, mesh=axed, in_specs=in_specs, out_specs=out_specs, check_vma=False
    )
```
